256 devices in a mesh: chan: 32 (over y_hi, z, core), hour: 8 (over y_lo, x).
Axes of the slice: x: 4, y: 4 (y_hi: 2, y_lo: 2; y = y_hi * 2 + y_lo), z: 8, core: 2. Of those that a mesh axis runs over, the one named last changes fastest.
Arguments:
- spectra: float32 [48, 256, 2, 4096], P('hour', 'chan'), may hold values from -2.5 to 2.5
- smooth_kernel: bfloat16 [3, 32, 128, 128], P(None, 'hour'), may hold values from -0.3125 to 0.3125
- owner_ids: int32 [4], replicated, may hold values from 0 to 31, as said below
- turn_order: int32 [4], replicated, may hold values from 0 to 3, each once
- source_pick: int32 [1024], P('chan'), may hold values from 0 to 7
- receiver_pick: int32 [1024], P('chan'), may hold values from 0 to 7
Outputs:
- correlations: bfloat16 [4, 1024, 2, 4096], P(None, 'chan', None, 'hour')
The draws below stay inside these ranges and needn't reach their ends.
Inputs may be any that keep to these rules, and one draw needn't show every extreme that they name: `owner_ids`: distinct indices along chan.
All inputs are finite; a program needn't handle non-finite values.
Results may differ from the reference program's by a relative error of at most 0.0049.
Values may be sent and summed in bfloat16 or wider, within the bound.
A program may use at most 128 MiB of HBM per device.

```python
import jax
import jax.numpy as jnp
from jax import lax

F = 4096
BAND = 128
TURNS = 4
C_DEV = 8
PAIRS = 32
CHANNELS = 256
HOURS = 48
PAIRS_ALL = 1024
NB = 32
N_CHAN = 32


def draw_owner_ids(key, part):
    key = jax.random.fold_in(key, 7)
    middle_key = jax.random.fold_in(key, 1)
    order_key = jax.random.fold_in(key, 2)
    middle = 1 + jax.random.permutation(middle_key, N_CHAN - 2)[:TURNS - 2]
    ends = jnp.array([0, N_CHAN - 1], dtype=jnp.int32)
    values = jnp.concatenate([ends, middle.astype(jnp.int32)])
    placing = jax.random.permutation(order_key, TURNS)
    return values[placing].astype(jnp.int32)


def place_ends(values, key, smallest, largest):
    shape = values.shape
    index_at = [jax.random.randint(jax.random.fold_in(key, axis), (), 0, shape[axis]) for axis in range(len(shape))]
    values = values.at[tuple(index_at)].set(smallest)
    longest = shape.index(max(shape))
    index_at[longest] = (index_at[longest] + 1) % shape[longest]
    return values.at[tuple(index_at)].set(largest)


def steps_of(own_key, shape, pieces, least, largest):
    level, own = 1.0, jax.random.fold_in(own_key, 6)
    for axis_at, parts in pieces:
        draws = jnp.exp(jax.random.uniform(jax.random.fold_in(own, axis_at), (parts,), jnp.float32, least / len(pieces), largest / len(pieces)))
        level = level * jnp.repeat(draws, shape[axis_at] // parts).reshape([-1 if axis == axis_at else 1 for axis in range(len(shape))])
    return level


def centred(stream_key, extent, width, reach, shards=(), held_as=jnp.bfloat16):
    factor_of = steps_of(stream_key, extent, shards, -0.22, 0.18) if shards else 1.0
    values = jax.random.normal(stream_key, extent, jnp.float32) * width * factor_of
    return jnp.minimum(jnp.maximum(values, -reach), reach).astype(held_as)


def setup_inputs(seed: int = 0) -> dict:
    seeds = jax.random.split(jax.random.key(seed), 7)
    return {
        "spectra": centred(seeds[0], (HOURS, CHANNELS, 2, F), 0.35, 2.5, ((0, 8), (1, 32)), jnp.float32),
        "smooth_kernel": centred(seeds[1], (3, NB, BAND, BAND), (3 * BAND) ** -0.5, 0.3125, ((1, 8),)),
        "owner_ids": draw_owner_ids(jax.random.fold_in(seeds[6], 71), 0),
        "turn_order": jax.random.permutation(seeds[3], TURNS).astype(jnp.int32),
        "source_pick": place_ends(jax.random.randint(seeds[4], (PAIRS_ALL,), 0, C_DEV), jax.random.fold_in(seeds[4], 1), 0, C_DEV - 1).astype(jnp.int32),
        "receiver_pick": place_ends(jax.random.randint(seeds[5], (PAIRS_ALL,), 0, C_DEV), jax.random.fold_in(seeds[5], 1), 0, C_DEV - 1).astype(jnp.int32),
    }


def correlate(source_block, receiver_block, source_index, receiver_index):
    source_rows = jnp.take(source_block, source_index, axis=1)
    receiver_rows = jnp.take(receiver_block, receiver_index, axis=1)
    source_real = source_rows[:, :, 0]
    source_imag = source_rows[:, :, 1]
    receiver_real = receiver_rows[:, :, 0]
    receiver_imag = receiver_rows[:, :, 1]
    real_part = jnp.sum(source_real * receiver_real + source_imag * receiver_imag, axis=0)
    imag_part = jnp.sum(source_imag * receiver_real - source_real * receiver_imag, axis=0)
    return jnp.stack([real_part, imag_part], axis=1)


def smooth(stacked, kernel):
    block_count = kernel.shape[1]
    pad_width = [(0, 0)] * (stacked.ndim - 1) + [(BAND, BAND)]
    padded = jnp.pad(stacked, pad_width)
    blocks = padded.reshape(stacked.shape[:-1] + (block_count + 2, BAND)).astype(jnp.float32)
    summed = jnp.zeros(stacked.shape[:-1] + (block_count, BAND), jnp.float32)
    for offset in range(3):
        window = blocks[..., offset:offset + block_count, :]
        summed = summed + jnp.einsum("...ia,iab->...ib", window, kernel[offset].astype(jnp.float32), precision=lax.Precision.HIGHEST)
    return summed.reshape(stacked.shape).astype(jnp.bfloat16)


def reference(spectra, smooth_kernel, owner_ids, turn_order, source_pick, receiver_pick):
    group_count = spectra.shape[1] // C_DEV
    bins = spectra.shape[3]
    grouped = spectra.reshape(spectra.shape[0], group_count, C_DEV, 2, bins)
    source_groups = source_pick.reshape(group_count, PAIRS)
    receiver_groups = receiver_pick.reshape(group_count, PAIRS)
    outputs = []
    for turn_index in range(TURNS):
        owner_index = owner_ids[turn_order[turn_index]].astype(jnp.int32)
        source_block = lax.dynamic_index_in_dim(grouped, owner_index, axis=1, keepdims=False)

        def one_group(items):
            group_index, source_row, receiver_row = items
            receiver_block = lax.dynamic_index_in_dim(grouped, group_index, axis=1, keepdims=False)
            return correlate(source_block, receiver_block, source_row, receiver_row)

        stacked = lax.map(one_group, (jnp.arange(group_count, dtype=jnp.int32), source_groups, receiver_groups))
        stacked = stacked.reshape(group_count * PAIRS, 2, bins).astype(jnp.bfloat16)
        outputs.append(smooth(stacked, smooth_kernel))
    return jnp.stack(outputs, axis=0)
```

```python
import jax
import jax.numpy as jnp
from jax import lax
from jax.experimental import pallas as pl
from jax.experimental.pallas import tpu as pltpu
from jax.sharding import PartitionSpec as P

MESH = pl.DeviceIdType.MESH

BAND = 128
TURNS = 4
C_DEV = 8
PAIRS = 32
HOUR_DEVS = 8
HOURS_DEV = 6
Z = 8
GROUPS = 4
ROWS = HOURS_DEV * 16
NB = 32
BF16 = jnp.bfloat16
F32 = jnp.float32


def body(
    spectra, kernel, owner_ids, turn_order, source_pick, receiver_pick, out,
    raw, staged, recv, up, down, chosen, acc, onehot, picked, halo, merged,
    raw_sem, a2a_send, a2a_recv, up_send, up_recv, down_send, down_recv,
    hot_send, hot_recv, out_send, out_recv, edge_send, self_sem,
):
    chan = lax.axis_index("chan")
    hour = lax.axis_index("hour")
    core = chan % 2
    z = (chan // 2) % Z
    y_hi = chan // (2 * Z)
    group = y_hi * 2 + core

    def chan_of(g, level):
        return ((g // 2) * Z + level) * 2 + g % 2

    load = pltpu.make_async_copy(spectra, raw, raw_sem)
    load.start()

    barrier = pltpu.get_barrier_semaphore()

    def greet(n, _):
        g, h = n // HOUR_DEVS, n % HOUR_DEVS

        @pl.when(jnp.logical_or(g != group, h != hour))
        def _():
            pl.semaphore_signal(
                barrier, inc=1, device_id=(chan_of(g, z), h), device_id_type=MESH
            )

        return 0

    above = chan_of(group, (z + 1) % Z)
    below = chan_of(group, (z + Z - 1) % Z)
    lax.fori_loop(0, NB, greet, 0)
    pl.semaphore_signal(barrier, inc=1, device_id=(above, hour), device_id_type=MESH)
    pl.semaphore_signal(barrier, inc=1, device_id=(below, hour), device_id_type=MESH)

    src = source_pick[...]
    rec = receiver_pick[...]
    code = (((rec - src) & 7) * 16 + src).astype(F32)
    row = lax.broadcasted_iota(jnp.int32, (PAIRS, PAIRS), 0)
    col = lax.broadcasted_iota(jnp.int32, (PAIRS, PAIRS), 1)
    spread = jnp.where(row == col, jnp.broadcast_to(code, (PAIRS, PAIRS)), 0.0)
    code_col = jnp.sum(spread, axis=1, keepdims=True)
    lane = lax.broadcasted_iota(jnp.int32, (PAIRS, BAND), 1).astype(F32)
    for c in range(2):
        hot = jnp.where(lane == code_col + 8.0 * c, 1.0, 0.0)
        onehot[group, pl.ds(c * PAIRS, PAIRS), :] = hot.astype(BF16)

    acc[...] = jnp.zeros_like(acc)

    @pl.when(hour == 0)
    def _():
        halo[0] = jnp.zeros((2 * TURNS * PAIRS, BAND), BF16)

    @pl.when(hour == HOUR_DEVS - 1)
    def _():
        halo[5] = jnp.zeros((2 * TURNS * PAIRS, BAND), BF16)

    load.wait()
    pl.semaphore_wait(barrier, NB + 1)

    def a2a(g, h):
        band = h * GROUPS + g
        return pltpu.make_async_remote_copy(
            src_ref=staged.at[band],
            dst_ref=recv.at[group, hour],
            send_sem=a2a_send.at[band],
            recv_sem=a2a_recv.at[group, hour],
            device_id=(chan_of(g, z), h),
            device_id_type=MESH,
        )

    def scatter(n, _):
        k = n // GROUPS
        g = (group + n) % GROUPS
        step = (k + 1) // 2
        shift = jnp.where(k % 2 == 1, step, 2 * Z - step)
        h = (hour + 4 * Z - z - shift) % HOUR_DEVS
        band = h * GROUPS + g
        mine = jnp.logical_and(g == group, h == hour)
        for i in range(HOURS_DEV):
            parts = [
                raw[pl.ds(i * 512 + band * 2 + p, 8, stride=64), :] for p in range(2)
            ]
            staged[band, pl.ds(i * 16, 16), :] = jnp.concatenate(parts, 0).astype(BF16)

        @pl.when(jnp.logical_not(mine))
        def _():
            a2a(g, h).start()

        @pl.when(mine)
        def _():
            recv[group, hour] = staged[band]

        return 0

    lax.fori_loop(0, NB, scatter, 0)

    def hot_copy(g):
        return pltpu.make_async_remote_copy(
            src_ref=onehot.at[group],
            dst_ref=onehot.at[group],
            send_sem=hot_send.at[g],
            recv_sem=hot_recv.at[group],
            device_id=(chan_of(g, z), hour),
            device_id_type=MESH,
        )

    def hot_wait(g):
        return pltpu.make_async_remote_copy(
            src_ref=onehot.at[group],
            dst_ref=onehot.at[g],
            send_sem=hot_send.at[g],
            recv_sem=hot_recv.at[g],
            device_id=(chan_of(g, z), hour),
            device_id_type=MESH,
        )

    def others(fn):
        def each(n, _):
            fn((group + n) % GROUPS)
            return 0

        lax.fori_loop(1, GROUPS, each, 0)

    others(lambda g: hot_copy(g).start())

    owners = [owner_ids[turn_order[t]] for t in range(TURNS)]
    owner_z = [(o // 2) % Z for o in owners]
    owner_g = [(o // (2 * Z)) * 2 + o % 2 for o in owners]

    def wait_pieces(h):
        def each(g, _):
            @pl.when(jnp.logical_or(g != group, h != hour))
            def _():
                pltpu.make_async_remote_copy(
                    src_ref=staged.at[0],
                    dst_ref=recv.at[g, h],
                    send_sem=a2a_send.at[0],
                    recv_sem=a2a_recv.at[g, h],
                    device_id=(chan_of(g, z), h),
                    device_id_type=MESH,
                ).wait_recv()

            return 0

        lax.fori_loop(0, GROUPS, each, 0)

    def merge(buf, s, h, first):
        for i in range(HOURS_DEV):
            rows = pl.ds(i * 16, 16)
            held = [recv[g, h, rows, :].astype(F32) for g in range(GROUPS)]
            for t in range(TURNS):
                mine = held[0]
                for g in range(1, GROUPS):
                    mine = lax.select_n(owner_g[t] == g, mine, held[g])
                if not first:
                    mine = lax.select_n(
                        owner_z[t] == z, buf[s, t, rows, :].astype(F32), mine
                    )
                buf[s, t, rows, :] = mine.astype(BF16)

    def hop(buf, s, send, arrive, target):
        return pltpu.make_async_remote_copy(
            src_ref=buf.at[s],
            dst_ref=buf.at[s + 1],
            send_sem=send.at[s],
            recv_sem=arrive.at[s + 1],
            device_id=(target, hour),
            device_id_type=MESH,
        )

    def arrived(buf, s, send, arrive, source):
        pltpu.make_async_remote_copy(
            src_ref=buf.at[0],
            dst_ref=buf.at[s],
            send_sem=send.at[0],
            recv_sem=arrive.at[s],
            device_id=(source, hour),
            device_id_type=MESH,
        ).wait_recv()

    def hour_of(q):
        return (q + hour + 4 * Z) % HOUR_DEVS

    def choose(r, slot):
        q = z - r + 2 * Z
        for t in range(TURNS):
            position = (owner_z[t] + 4 * Z - q) % Z
            lower = position < jnp.maximum(r, 1)
            for i in range(HOURS_DEV):
                rows = pl.ds(i * 16, 16)
                value = lax.select_n(
                    lower,
                    down[Z - 1 - r, t, rows, :].astype(F32),
                    up[r, t, rows, :].astype(F32),
                )
                chosen[t, slot, rows, :] = value

    def multiply(g, t0, hours):
        start = tuple(
            acc[g, t0 + t, k, c] for t in range(2) for k in range(8) for c in range(2)
        )

        def each(n, sums):
            slot, i = n // HOURS_DEV, n % HOURS_DEV
            h = jnp.where(slot == 0, hours[0], hours[1])
            rows = pl.ds(pl.multiple_of(i * 16, 16), 16)
            b = recv[g, h, rows, :].astype(F32)
            b0, b1 = b[:8], b[8:]
            a = [chosen[t0 + t, slot, rows, :] for t in range(2)]
            new = list(sums)
            for k in range(8):
                r0 = pltpu.roll(b0, 8 - k, 0) if k else b0
                r1 = pltpu.roll(b1, 8 - k, 0) if k else b1
                for t in range(2):
                    a0, a1 = a[t][:8], a[t][8:]
                    at = (t * 8 + k) * 2
                    new[at] = new[at] + (a0 * r0 + a1 * r1)
                    new[at + 1] = new[at + 1] + (a1 * r0 - a0 * r1)
            return tuple(new)

        sums = lax.fori_loop(0, 2 * HOURS_DEV, each, start)
        n = 0
        for t in range(2):
            for k in range(8):
                for c in range(2):
                    acc[g, t0 + t, k, c] = sums[n]
                    n += 1

    def step(s, first, send):
        low, high = hour_of(z - s), hour_of(z + 1 + s)
        if not first:
            arrived(up, s, up_send, up_recv, below)
        if send:
            merge(up, s, low, first)
            hop(up, s, up_send, up_recv, above).start()
        if not first:
            arrived(down, s, down_send, down_recv, above)
        if send:
            merge(down, s, high, first)
            hop(down, s, down_send, down_recv, below).start()
        return low, high

    def early(s, _):
        wait_pieces(hour_of(z - s))
        wait_pieces(hour_of(z + 1 + s))
        step(s, False, True)
        return 0

    def late(s, _):
        low, high = step(s, False, True)
        choose(s, 0)
        choose(Z - 1 - s, 1)

        def each(n, _):
            multiply(n // 2, (n % 2) * 2, (low, high))
            return 0

        lax.fori_loop(0, GROUPS * 2, each, 0)
        return 0

    wait_pieces(hour_of(z))
    wait_pieces(hour_of(z + 1))
    step(0, True, True)
    lax.fori_loop(1, 4, early, 0)
    lax.fori_loop(4, Z - 1, late, 0)
    low, high = step(Z - 1, False, False)
    choose(Z - 1, 0)
    choose(0, 1)
    others(lambda g: hot_wait(g).wait_recv())

    def deliver(g):
        return pltpu.make_async_remote_copy(
            src_ref=picked.at[g],
            dst_ref=halo.at[1 + group],
            send_sem=out_send.at[g],
            recv_sem=out_recv.at[1 + group],
            device_id=(chan_of(g, z), hour),
            device_id_type=MESH,
        )

    def edge(g, to, slot):
        return pltpu.make_async_remote_copy(
            src_ref=picked.at[g],
            dst_ref=halo.at[slot],
            send_sem=edge_send.at[g],
            recv_sem=out_recv.at[slot],
            device_id=(chan_of(g, z), to),
            device_id_type=MESH,
        )

    to_low = jnp.logical_and(group == 0, hour > 0)
    to_high = jnp.logical_and(group == GROUPS - 1, hour < HOUR_DEVS - 1)

    def finish(n, _):
        g = (group + 1 + n) % GROUPS
        multiply(g, 0, (low, high))
        multiply(g, 2, (low, high))
        for t in range(TURNS):
            table = jnp.concatenate(
                [acc[g, t, k, c] for k in range(8) for c in range(2)], axis=0
            ).astype(BF16)
            rows = jnp.dot(onehot[g], table, preferred_element_type=F32)
            picked[g, pl.ds(t * 2 * PAIRS, 2 * PAIRS), :] = rows.astype(BF16)

        @pl.when(g != group)
        def _():
            deliver(g).start()

        @pl.when(g == group)
        def _():
            halo[1 + group] = picked[g]

        @pl.when(to_low)
        def _():
            edge(g, hour - 1, 5).start()

        @pl.when(to_high)
        def _():
            edge(g, hour + 1, 0).start()

        return 0

    lax.fori_loop(0, GROUPS, finish, 0)

    def out_wait(slot):
        pltpu.make_async_remote_copy(
            src_ref=picked.at[0],
            dst_ref=halo.at[slot],
            send_sem=out_send.at[0],
            recv_sem=out_recv.at[slot],
            device_id=(chan, hour),
            device_id_type=MESH,
        ).wait_recv()

    others(lambda g: out_wait(1 + g))

    @pl.when(hour > 0)
    def _():
        out_wait(0)

    @pl.when(hour < HOUR_DEVS - 1)
    def _():
        out_wait(5)

    for b in range(4):
        total = jnp.dot(halo[b], kernel[0, b], preferred_element_type=F32)
        for d in range(1, 3):
            total += jnp.dot(halo[b + d], kernel[d, b], preferred_element_type=F32)
        for t in range(TURNS):
            for c in range(2):
                for p in range(0, PAIRS, 8):
                    at = t * 2 * PAIRS + c * PAIRS + p
                    merged[pl.ds((t * PAIRS + p) * 8 + b * 2 + c, 8, stride=8), :] = (
                        total[at : at + 8]
                    )
    out[...] = merged[...].astype(BF16)

    def drain(n, _):
        g, h = n // HOUR_DEVS, n % HOUR_DEVS

        @pl.when(jnp.logical_or(g != group, h != hour))
        def _():
            a2a(g, h).wait_send()

        return 0

    lax.fori_loop(0, NB, drain, 0)
    others(lambda g: hot_copy(g).wait_send())
    others(lambda g: deliver(g).wait_send())

    def drain_hops(s, _):
        hop(up, s, up_send, up_recv, above).wait_send()
        hop(down, s, down_send, down_recv, below).wait_send()
        return 0

    lax.fori_loop(0, Z - 1, drain_hops, 0)

    @pl.when(jnp.logical_or(to_low, to_high))
    def _():
        def each(g, _):
            edge(g, hour, 0).wait_send()
            return 0

        lax.fori_loop(0, GROUPS, each, 0)


def local(spectra, smooth_kernel, owner_ids, turn_order, source_pick, receiver_pick):
    tiles = spectra.reshape(HOURS_DEV, C_DEV, 2, NB, BAND)
    tiles = tiles.transpose(0, 1, 3, 2, 4).reshape(HOURS_DEV * C_DEV * NB * 2, BAND)
    vmem = pl.BlockSpec(memory_space=pltpu.VMEM)
    smem = pl.BlockSpec(memory_space=pltpu.SMEM)
    rows = TURNS * 2 * PAIRS
    dma = pltpu.SemaphoreType.DMA
    result = pl.pallas_call(
        body,
        out_shape=jax.ShapeDtypeStruct((rows * 4, BAND), BF16),
        in_specs=[pl.BlockSpec(memory_space=pl.ANY), vmem, smem, smem, vmem, vmem],
        out_specs=vmem,
        scratch_shapes=[
            pltpu.VMEM((HOURS_DEV * C_DEV * NB * 2, BAND), F32),
            pltpu.VMEM((NB, ROWS, BAND), BF16),
            pltpu.VMEM((GROUPS, HOUR_DEVS, ROWS, BAND), BF16),
            pltpu.VMEM((Z, TURNS, ROWS, BAND), BF16),
            pltpu.VMEM((Z, TURNS, ROWS, BAND), BF16),
            pltpu.VMEM((TURNS, 2, ROWS, BAND), F32),
            pltpu.VMEM((GROUPS, TURNS, 8, 2, 8, BAND), F32),
            pltpu.VMEM((GROUPS, 2 * PAIRS, BAND), BF16),
            pltpu.VMEM((GROUPS, rows, BAND), BF16),
            pltpu.VMEM((6, rows, BAND), BF16),
            pltpu.VMEM((rows * 4, BAND), F32),
            dma,
            dma((NB,)),
            dma((GROUPS, HOUR_DEVS)),
            dma((Z,)),
            dma((Z,)),
            dma((Z,)),
            dma((Z,)),
            dma((GROUPS,)),
            dma((GROUPS,)),
            dma((GROUPS,)),
            dma((6,)),
            dma((GROUPS,)),
            dma,
        ],
        compiler_params=pltpu.CompilerParams(
            collective_id=0, has_side_effects=True, vmem_limit_bytes=48 * 1024 * 1024
        ),
    )(
        tiles,
        smooth_kernel,
        owner_ids,
        turn_order,
        source_pick.reshape(1, PAIRS),
        receiver_pick.reshape(1, PAIRS),
    )
    result = result.reshape(TURNS, PAIRS, 4, 2, BAND).transpose(0, 1, 3, 2, 4)
    return result.reshape(TURNS, PAIRS, 2, 4 * BAND)


def solution(mesh):
    return jax.shard_map(
        local,
        mesh=mesh,
        in_specs=(
            P("hour", "chan", None, None),
            P(None, "hour", None, None),
            P(),
            P(),
            P("chan"),
            P("chan"),
        ),
        out_specs=P(None, "chan", None, "hour"),
        check_vma=False,
    )
```

```python
import jax
import jax.numpy as jnp
from jax import lax
from jax.experimental import pallas as pl
from jax.experimental.pallas import tpu as pltpu
from jax.sharding import PartitionSpec as P

MESH = pl.DeviceIdType.MESH

BAND = 128
TURNS = 4
C_DEV = 8
PAIRS = 32
HOUR_DEVS = 8
HOURS_DEV = 6
Z = 8
GROUPS = 4
ROWS = HOURS_DEV * 16
TG = 2
PARTS = TURNS // TG
NB = 32
BF16 = jnp.bfloat16
F32 = jnp.float32


def body(
    spectra, kernel_hbm, owners_hbm, order_hbm, source_pick, receiver_pick, out,
    raw, staged, recv, up, down, chosen, acc, onehot, picked, halo, merged,
    kernel, owner_ids, turn_order, load_sem,
    a2a_send, a2a_recv, up_send, up_recv, down_send, down_recv,
    hot_send, hot_recv, out_send, out_recv, edge_send,
):
    chan = lax.axis_index("chan")
    hour = lax.axis_index("hour")
    core = chan % 2
    z = (chan // 2) % Z
    y_hi = chan // (2 * Z)
    group = y_hi * 2 + core

    def chan_of(g, level):
        return ((g // 2) * Z + level) * 2 + g % 2

    loads = [
        pltpu.make_async_copy(a, b, load_sem.at[n])
        for n, (a, b) in enumerate(
            [
                (spectra, raw),
                (owners_hbm, owner_ids),
                (order_hbm, turn_order),
                (kernel_hbm, kernel),
            ]
        )
    ]
    for load in loads:
        load.start()

    barrier = pltpu.get_barrier_semaphore()

    def greet(n, _):
        g, h = n // HOUR_DEVS, n % HOUR_DEVS

        @pl.when(jnp.logical_or(g != group, h != hour))
        def _():
            pl.semaphore_signal(
                barrier, inc=1, device_id=(chan_of(g, z), h), device_id_type=MESH
            )

        return 0

    above = chan_of(group, (z + 1) % Z)
    below = chan_of(group, (z + Z - 1) % Z)
    lax.fori_loop(0, NB, greet, 0)
    pl.semaphore_signal(barrier, inc=1, device_id=(above, hour), device_id_type=MESH)
    pl.semaphore_signal(barrier, inc=1, device_id=(below, hour), device_id_type=MESH)

    src = source_pick[...]
    rec = receiver_pick[...]
    code = (((rec - src) & 7) * 16 + src).astype(F32)
    row = lax.broadcasted_iota(jnp.int32, (PAIRS, PAIRS), 0)
    col = lax.broadcasted_iota(jnp.int32, (PAIRS, PAIRS), 1)
    spread = jnp.where(row == col, jnp.broadcast_to(code, (PAIRS, PAIRS)), 0.0)
    code_col = jnp.sum(spread, axis=1, keepdims=True)
    lane = lax.broadcasted_iota(jnp.int32, (PAIRS, BAND), 1).astype(F32)
    for c in range(2):
        hot = jnp.where(lane == code_col + 8.0 * c, 1.0, 0.0)
        onehot[group, pl.ds(c * PAIRS, PAIRS), :] = hot.astype(BF16)

    acc[...] = jnp.zeros_like(acc)

    @pl.when(hour == 0)
    def _():
        halo[0] = jnp.zeros((2 * TURNS * PAIRS, BAND), BF16)

    @pl.when(hour == HOUR_DEVS - 1)
    def _():
        halo[5] = jnp.zeros((2 * TURNS * PAIRS, BAND), BF16)

    for load in loads[:3]:
        load.wait()
    pl.semaphore_wait(barrier, NB + 1)

    def a2a(g, h):
        band = h * GROUPS + g
        return pltpu.make_async_remote_copy(
            src_ref=staged.at[band],
            dst_ref=recv.at[group, hour],
            send_sem=a2a_send.at[band],
            recv_sem=a2a_recv.at[group, hour],
            device_id=(chan_of(g, z), h),
            device_id_type=MESH,
        )

    def scatter(n, _):
        k = n // GROUPS
        g = (group + n) % GROUPS
        step = (k + 1) // 2
        shift = jnp.where(k % 2 == 1, step, 2 * Z - step)
        h = (hour + 4 * Z - z - shift) % HOUR_DEVS
        band = h * GROUPS + g
        mine = jnp.logical_and(g == group, h == hour)
        for i in range(HOURS_DEV):
            parts = [
                raw[pl.ds(i * 512 + band * 2 + p, 8, stride=64), :] for p in range(2)
            ]
            staged[band, pl.ds(i * 16, 16), :] = jnp.concatenate(parts, 0).astype(BF16)

        @pl.when(jnp.logical_not(mine))
        def _():
            a2a(g, h).start()

        @pl.when(mine)
        def _():
            recv[group, hour] = staged[band]

        return 0

    lax.fori_loop(0, NB, scatter, 0)

    def hot_copy(g):
        return pltpu.make_async_remote_copy(
            src_ref=onehot.at[group],
            dst_ref=onehot.at[group],
            send_sem=hot_send.at[g],
            recv_sem=hot_recv.at[group],
            device_id=(chan_of(g, z), hour),
            device_id_type=MESH,
        )

    def hot_wait(g):
        return pltpu.make_async_remote_copy(
            src_ref=onehot.at[group],
            dst_ref=onehot.at[g],
            send_sem=hot_send.at[g],
            recv_sem=hot_recv.at[g],
            device_id=(chan_of(g, z), hour),
            device_id_type=MESH,
        )

    def others(fn):
        def each(n, _):
            fn((group + n) % GROUPS)
            return 0

        lax.fori_loop(1, GROUPS, each, 0)


    owners = [owner_ids[turn_order[t]] for t in range(TURNS)]
    owner_z = [(o // 2) % Z for o in owners]
    owner_g = [(o // (2 * Z)) * 2 + o % 2 for o in owners]

    def wait_pieces(h):
        def each(g, _):
            @pl.when(jnp.logical_or(g != group, h != hour))
            def _():
                pltpu.make_async_remote_copy(
                    src_ref=staged.at[0],
                    dst_ref=recv.at[g, h],
                    send_sem=a2a_send.at[0],
                    recv_sem=a2a_recv.at[g, h],
                    device_id=(chan_of(g, z), h),
                    device_id_type=MESH,
                ).wait_recv()

            return 0

        lax.fori_loop(0, GROUPS, each, 0)

    def merge(buf, s, h, t0, first):
        for i in range(HOURS_DEV):
            rows = pl.ds(i * 16, 16)
            held = [recv[g, h, rows, :] for g in range(GROUPS)]
            for t in range(t0, t0 + TG):
                mine = held[0]
                for g in range(1, GROUPS):
                    mine = lax.select_n(owner_g[t] == g, mine, held[g])
                if not first:
                    mine = lax.select_n(owner_z[t] == z, buf[s, t, rows, :], mine)
                buf[s, t, rows, :] = mine

    def hop(buf, s, part, send, arrive, target):
        turns = pl.ds(part * TG, TG)
        return pltpu.make_async_remote_copy(
            src_ref=buf.at[s, turns],
            dst_ref=buf.at[s + 1, turns],
            send_sem=send.at[s, part],
            recv_sem=arrive.at[s + 1, part],
            device_id=(target, hour),
            device_id_type=MESH,
        )

    def arrived(buf, s, part, send, arrive, source):
        turns = pl.ds(part * TG, TG)
        pltpu.make_async_remote_copy(
            src_ref=buf.at[0, turns],
            dst_ref=buf.at[s, turns],
            send_sem=send.at[0, part],
            recv_sem=arrive.at[s, part],
            device_id=(source, hour),
            device_id_type=MESH,
        ).wait_recv()

    def hour_of(q):
        return (q + hour + 4 * Z) % HOUR_DEVS

    def choose(r, slot, turns):
        q = z - r + 2 * Z
        for t in turns:
            position = (owner_z[t] + 4 * Z - q) % Z
            lower = position < jnp.maximum(r, 1)
            for i in range(HOURS_DEV):
                rows = pl.ds(i * 16, 16)
                value = lax.select_n(
                    lower, down[Z - 1 - r, t, rows, :], up[r, t, rows, :]
                )
                chosen[t, slot, rows, :] = value.astype(F32)

    def multiply(g, t0, hours):
        start = tuple(
            acc[g, t0 + t, k, c] for t in range(2) for k in range(8) for c in range(2)
        )

        def each(n, sums):
            slot, i = n // HOURS_DEV, n % HOURS_DEV
            h = hours[slot]
            rows = pl.ds(i * 16, 16)
            b = recv[g, h, rows, :].astype(F32)
            b0, b1 = b[:8], b[8:]
            a = [chosen[t0 + t, slot, rows, :] for t in range(2)]
            new = list(sums)
            for k in range(8):
                r0 = pltpu.roll(b0, 8 - k, 0) if k else b0
                r1 = pltpu.roll(b1, 8 - k, 0) if k else b1
                for t in range(2):
                    a0, a1 = a[t][:8], a[t][8:]
                    at = (t * 8 + k) * 2
                    new[at] = new[at] + (a0 * r0 + a1 * r1)
                    new[at + 1] = new[at + 1] + (a1 * r0 - a0 * r1)
            return tuple(new)

        sums = start
        for n in range(2 * HOURS_DEV):
            sums = each(n, sums)
        n = 0
        for t in range(2):
            for k in range(8):
                for c in range(2):
                    acc[g, t0 + t, k, c] = sums[n]
                    n += 1

    def step(s, first):
        low, high = hour_of(z - s), hour_of(z + 1 + s)
        for part in range(PARTS):
            if not first:
                arrived(up, s, part, up_send, up_recv, below)
            merge(up, s, low, part * TG, first)
            hop(up, s, part, up_send, up_recv, above).start()
            if not first:
                arrived(down, s, part, down_send, down_recv, above)
            merge(down, s, high, part * TG, first)
            hop(down, s, part, down_send, down_recv, below).start()
        return low, high

    def early(s, _):
        wait_pieces(hour_of(z - s))
        wait_pieces(hour_of(z + 1 + s))
        step(s, False)

        @pl.when(s == 1)
        def _():
            others(lambda g: hot_copy(g).start())

        return 0

    def late(s, _):
        low, high = step(s, False)
        choose(s, 0, range(TURNS))
        choose(Z - 1 - s, 1, range(TURNS))

        def each(n, _):
            multiply(n // 2, (n % 2) * 2, (low, high))
            return 0

        lax.fori_loop(0, GROUPS * 2, each, 0)
        return 0

    wait_pieces(hour_of(z))
    wait_pieces(hour_of(z + 1))
    step(0, True)
    lax.fori_loop(1, 4, early, 0)
    lax.fori_loop(4, Z - 1, late, 0)
    low, high = hour_of(z + 1), hour_of(z)
    others(lambda g: hot_wait(g).wait_recv())

    def deliver(g, part):
        rows = pl.ds(part * TG * 2 * PAIRS, TG * 2 * PAIRS)
        return pltpu.make_async_remote_copy(
            src_ref=picked.at[g, rows],
            dst_ref=halo.at[1 + group, rows],
            send_sem=out_send.at[g, part],
            recv_sem=out_recv.at[1 + group, part],
            device_id=(chan_of(g, z), hour),
            device_id_type=MESH,
        )

    def edge(g, part, to, slot):
        rows = pl.ds(part * TG * 2 * PAIRS, TG * 2 * PAIRS)
        return pltpu.make_async_remote_copy(
            src_ref=picked.at[g, rows],
            dst_ref=halo.at[slot, rows],
            send_sem=edge_send.at[g, part],
            recv_sem=out_recv.at[slot, part],
            device_id=(chan_of(g, z), to),
            device_id_type=MESH,
        )

    to_low = jnp.logical_and(group == 0, hour > 0)
    to_high = jnp.logical_and(group == GROUPS - 1, hour < HOUR_DEVS - 1)

    for part in range(PARTS):
        turns = range(part * TG, part * TG + TG)
        arrived(up, Z - 1, part, up_send, up_recv, below)
        arrived(down, Z - 1, part, down_send, down_recv, above)
        choose(Z - 1, 0, turns)
        choose(0, 1, turns)

        def finish(n, _, part=part, turns=turns):
            g = (group + 1 + n) % GROUPS
            for t in turns[::2]:
                multiply(g, t, (low, high))
            for t in turns:
                table = jnp.concatenate(
                    [acc[g, t, k, c] for k in range(8) for c in range(2)], axis=0
                ).astype(BF16)
                rows = jnp.dot(onehot[g], table, preferred_element_type=F32)
                picked[g, pl.ds(t * 2 * PAIRS, 2 * PAIRS), :] = rows.astype(BF16)

            @pl.when(g != group)
            def _():
                deliver(g, part).start()

            @pl.when(g == group)
            def _():
                rows = pl.ds(part * TG * 2 * PAIRS, TG * 2 * PAIRS)
                halo[1 + group, rows, :] = picked[g, rows, :]

            @pl.when(to_low)
            def _():
                edge(g, part, hour - 1, 5).start()

            @pl.when(to_high)
            def _():
                edge(g, part, hour + 1, 0).start()

            return 0

        lax.fori_loop(0, GROUPS, finish, 0)

    def out_wait(slot, part):
        rows = pl.ds(part * TG * 2 * PAIRS, TG * 2 * PAIRS)
        pltpu.make_async_remote_copy(
            src_ref=picked.at[0, rows],
            dst_ref=halo.at[slot, rows],
            send_sem=out_send.at[0, part],
            recv_sem=out_recv.at[slot, part],
            device_id=(chan, hour),
            device_id_type=MESH,
        ).wait_recv()

    loads[3].wait()
    for part in range(PARTS):
        others(lambda g: out_wait(1 + g, part))

        @pl.when(hour > 0)
        def _():
            out_wait(0, part)

        @pl.when(hour < HOUR_DEVS - 1)
        def _():
            out_wait(5, part)

        rows = pl.ds(part * TG * 2 * PAIRS, TG * 2 * PAIRS)
        for b in range(4):
            total = jnp.dot(halo[b, rows, :], kernel[0, b], preferred_element_type=F32)
            for d in range(1, 3):
                total += jnp.dot(
                    halo[b + d, rows, :], kernel[d, b], preferred_element_type=F32
                )
            for t in range(TG):
                for c in range(2):
                    for p in range(0, PAIRS, 8):
                        at = t * 2 * PAIRS + c * PAIRS + p
                        pair = (part * TG + t) * PAIRS + p
                        merged[pl.ds(pair * 8 + b * 2 + c, 8, stride=8), :] = total[
                            at : at + 8
                        ]
        done = pl.ds(part * TG * PAIRS * 8, TG * PAIRS * 8)
        out[done, :] = merged[done, :].astype(BF16)

    def drain(n, _):
        g, h = n // HOUR_DEVS, n % HOUR_DEVS

        @pl.when(jnp.logical_or(g != group, h != hour))
        def _():
            a2a(g, h).wait_send()

        return 0

    lax.fori_loop(0, NB, drain, 0)
    others(lambda g: hot_copy(g).wait_send())
    for part in range(PARTS):
        others(lambda g: deliver(g, part).wait_send())

    def drain_hops(s, _):
        for part in range(PARTS):
            hop(up, s, part, up_send, up_recv, above).wait_send()
            hop(down, s, part, down_send, down_recv, below).wait_send()
        return 0

    lax.fori_loop(0, Z - 1, drain_hops, 0)

    @pl.when(jnp.logical_or(to_low, to_high))
    def _():
        def each(g, _):
            for part in range(PARTS):
                edge(g, part, hour, 0).wait_send()
            return 0

        lax.fori_loop(0, GROUPS, each, 0)


def local(spectra, smooth_kernel, owner_ids, turn_order, source_pick, receiver_pick):
    tiles = spectra.reshape(HOURS_DEV, C_DEV, 2, NB, BAND)
    tiles = tiles.transpose(0, 1, 3, 2, 4).reshape(HOURS_DEV * C_DEV * NB * 2, BAND)
    vmem = pl.BlockSpec(memory_space=pltpu.VMEM)
    hbm = pl.BlockSpec(memory_space=pl.ANY)
    rows = TURNS * 2 * PAIRS
    dma = pltpu.SemaphoreType.DMA
    result = pl.pallas_call(
        body,
        out_shape=jax.ShapeDtypeStruct((rows * 4, BAND), BF16),
        in_specs=[hbm, hbm, hbm, hbm, vmem, vmem],
        out_specs=vmem,
        scratch_shapes=[
            pltpu.VMEM((HOURS_DEV * C_DEV * NB * 2, BAND), F32),
            pltpu.VMEM((NB, ROWS, BAND), BF16),
            pltpu.VMEM((GROUPS, HOUR_DEVS, ROWS, BAND), BF16),
            pltpu.VMEM((Z, TURNS, ROWS, BAND), BF16),
            pltpu.VMEM((Z, TURNS, ROWS, BAND), BF16),
            pltpu.VMEM((TURNS, 2, ROWS, BAND), F32),
            pltpu.VMEM((GROUPS, TURNS, 8, 2, 8, BAND), F32),
            pltpu.VMEM((GROUPS, 2 * PAIRS, BAND), BF16),
            pltpu.VMEM((GROUPS, rows, BAND), BF16),
            pltpu.VMEM((6, rows, BAND), BF16),
            pltpu.VMEM((rows * 4, BAND), F32),
            pltpu.VMEM((3, 4, BAND, BAND), BF16),
            pltpu.SMEM((TURNS,), jnp.int32),
            pltpu.SMEM((TURNS,), jnp.int32),
            dma((4,)),
            dma((NB,)),
            dma((GROUPS, HOUR_DEVS)),
            dma((Z, PARTS)),
            dma((Z, PARTS)),
            dma((Z, PARTS)),
            dma((Z, PARTS)),
            dma((GROUPS,)),
            dma((GROUPS,)),
            dma((GROUPS, PARTS)),
            dma((6, PARTS)),
            dma((GROUPS, PARTS)),
        ],
        compiler_params=pltpu.CompilerParams(
            collective_id=0, has_side_effects=True, vmem_limit_bytes=63 * 1024 * 1024
        ),
    )(
        tiles,
        smooth_kernel,
        owner_ids,
        turn_order,
        source_pick.reshape(1, PAIRS),
        receiver_pick.reshape(1, PAIRS),
    )
    result = result.reshape(TURNS, PAIRS, 4, 2, BAND).transpose(0, 1, 3, 2, 4)
    return result.reshape(TURNS, PAIRS, 2, 4 * BAND)


def solution(mesh):
    return jax.shard_map(
        local,
        mesh=mesh,
        in_specs=(
            P("hour", "chan", None, None),
            P(None, "hour", None, None),
            P(),
            P(),
            P("chan"),
            P("chan"),
        ),
        out_specs=P(None, "chan", None, "hour"),
        check_vma=False,
    )
```

```python
import jax
import jax.numpy as jnp
from jax import lax
from jax.experimental import pallas as pl
from jax.experimental.pallas import tpu as pltpu
from jax.sharding import PartitionSpec as P

MESH = pl.DeviceIdType.MESH

BAND = 128
TURNS = 4
C_DEV = 8
PAIRS = 32
HOUR_DEVS = 8
HOURS_DEV = 6
Z = 8
GROUPS = 4
ROWS = HOURS_DEV * 16
TG = 2
PARTS = TURNS // TG
FIRST = 32
PACED = 0
NB = 32
BF16 = jnp.bfloat16
F32 = jnp.float32


def body(
    spectra, kernel_hbm, owners_hbm, order_hbm, source_hbm, receiver_hbm, out,
    raw, staged, recv, up, down, chosen, acc, onehot, picked, halo, merged,
    kernel, owner_ids, turn_order, source_pick, receiver_pick, load_sem,
    a2a_send, a2a_recv, up_send, up_recv, down_send, down_recv,
    hot_send, hot_recv, out_send, out_recv, edge_send,
):
    chan = lax.axis_index("chan")
    hour = lax.axis_index("hour")
    core = chan % 2
    z = (chan // 2) % Z
    y_hi = chan // (2 * Z)
    group = y_hi * 2 + core

    def chan_of(g, level):
        return ((g // 2) * Z + level) * 2 + g % 2

    loads = [
        pltpu.make_async_copy(a, b, load_sem.at[n])
        for n, (a, b) in enumerate(
            [
                (spectra, raw),
                (owners_hbm, owner_ids),
                (order_hbm, turn_order),
                (source_hbm, source_pick),
                (receiver_hbm, receiver_pick),
                (kernel_hbm, kernel),
            ]
        )
    ]
    for load in loads:
        load.start()

    barrier = pltpu.get_barrier_semaphore()

    def greet(n, _):
        g, h = n // HOUR_DEVS, n % HOUR_DEVS

        @pl.when(jnp.logical_or(g != group, h != hour))
        def _():
            pl.semaphore_signal(
                barrier, inc=1, device_id=(chan_of(g, z), h), device_id_type=MESH
            )

        return 0

    above = chan_of(group, (z + 1) % Z)
    below = chan_of(group, (z + Z - 1) % Z)
    lax.fori_loop(0, NB, greet, 0)
    pl.semaphore_signal(barrier, inc=1, device_id=(above, hour), device_id_type=MESH)
    pl.semaphore_signal(barrier, inc=1, device_id=(below, hour), device_id_type=MESH)

    for load in loads[3:5]:
        load.wait()

    src = source_pick[...]
    rec = receiver_pick[...]
    code = (((rec - src) & 7) * 16 + src).astype(F32)
    row = lax.broadcasted_iota(jnp.int32, (PAIRS, PAIRS), 0)
    col = lax.broadcasted_iota(jnp.int32, (PAIRS, PAIRS), 1)
    spread = jnp.where(row == col, jnp.broadcast_to(code, (PAIRS, PAIRS)), 0.0)
    code_col = jnp.sum(spread, axis=1, keepdims=True)
    lane = lax.broadcasted_iota(jnp.int32, (PAIRS, BAND), 1).astype(F32)
    for c in range(2):
        hot = jnp.where(lane == code_col + 8.0 * c, 1.0, 0.0)
        onehot[group, pl.ds(c * PAIRS, PAIRS), :] = hot.astype(BF16)

    acc[...] = jnp.zeros_like(acc)

    @pl.when(hour == 0)
    def _():
        halo[0] = jnp.zeros((2 * TURNS * PAIRS, BAND), BF16)

    @pl.when(hour == HOUR_DEVS - 1)
    def _():
        halo[5] = jnp.zeros((2 * TURNS * PAIRS, BAND), BF16)

    for load in loads[:3]:
        load.wait()
    pl.semaphore_wait(barrier, NB + 1)

    def a2a(g, h):
        band = h * GROUPS + g
        return pltpu.make_async_remote_copy(
            src_ref=staged.at[band],
            dst_ref=recv.at[group, hour],
            send_sem=a2a_send.at[band],
            recv_sem=a2a_recv.at[group, hour],
            device_id=(chan_of(g, z), h),
            device_id_type=MESH,
        )

    def target(n):
        k = n // GROUPS
        g = (group + n) % GROUPS
        step = (k + 1) // 2
        shift = jnp.where(k % 2 == 1, step, 2 * Z - step)
        return g, (hour + 4 * Z - z - shift) % HOUR_DEVS

    def scatter(n, _):
        g, h = target(n)
        band = h * GROUPS + g
        mine = jnp.logical_and(g == group, h == hour)
        for i in range(HOURS_DEV):
            parts = [
                raw[pl.ds(i * 512 + band * 2 + p, 8, stride=64), :] for p in range(2)
            ]
            staged[band, pl.ds(i * 16, 16), :] = jnp.concatenate(parts, 0).astype(BF16)

        @pl.when(jnp.logical_not(mine))
        def _():
            a2a(g, h).start()

        @pl.when(mine)
        def _():
            recv[group, hour] = staged[band]

        return 0

    def drain(n, _):
        g, h = target(n)

        @pl.when(jnp.logical_or(g != group, h != hour))
        def _():
            a2a(g, h).wait_send()

        return 0

    lax.fori_loop(0, FIRST, scatter, 0)
    lax.fori_loop(0, PACED, drain, 0)
    lax.fori_loop(FIRST, NB, scatter, 0)

    def hot_copy(g):
        return pltpu.make_async_remote_copy(
            src_ref=onehot.at[group],
            dst_ref=onehot.at[group],
            send_sem=hot_send.at[g],
            recv_sem=hot_recv.at[group],
            device_id=(chan_of(g, z), hour),
            device_id_type=MESH,
        )

    def hot_wait(g):
        return pltpu.make_async_remote_copy(
            src_ref=onehot.at[group],
            dst_ref=onehot.at[g],
            send_sem=hot_send.at[g],
            recv_sem=hot_recv.at[g],
            device_id=(chan_of(g, z), hour),
            device_id_type=MESH,
        )

    def others(fn):
        def each(n, _):
            fn((group + n) % GROUPS)
            return 0

        lax.fori_loop(1, GROUPS, each, 0)


    owners = [owner_ids[turn_order[t]] for t in range(TURNS)]
    owner_z = [(o // 2) % Z for o in owners]
    owner_g = [(o // (2 * Z)) * 2 + o % 2 for o in owners]

    def wait_pieces(h):
        def each(g, _):
            @pl.when(jnp.logical_or(g != group, h != hour))
            def _():
                pltpu.make_async_remote_copy(
                    src_ref=staged.at[0],
                    dst_ref=recv.at[g, h],
                    send_sem=a2a_send.at[0],
                    recv_sem=a2a_recv.at[g, h],
                    device_id=(chan_of(g, z), h),
                    device_id_type=MESH,
                ).wait_recv()

            return 0

        lax.fori_loop(0, GROUPS, each, 0)

    def merge(buf, s, h, t0, first):
        for i in range(HOURS_DEV):
            rows = pl.ds(i * 16, 16)
            held = [recv[g, h, rows, :] for g in range(GROUPS)]
            for t in range(t0, t0 + TG):
                mine = held[0]
                for g in range(1, GROUPS):
                    mine = lax.select_n(owner_g[t] == g, mine, held[g])
                if not first:
                    mine = lax.select_n(owner_z[t] == z, buf[s, t, rows, :], mine)
                buf[s, t, rows, :] = mine

    def hop(buf, s, part, send, arrive, target):
        turns = pl.ds(part * TG, TG)
        return pltpu.make_async_remote_copy(
            src_ref=buf.at[s, turns],
            dst_ref=buf.at[s + 1, turns],
            send_sem=send.at[s, part],
            recv_sem=arrive.at[s + 1, part],
            device_id=(target, hour),
            device_id_type=MESH,
        )

    def arrived(buf, s, part, send, arrive, source):
        turns = pl.ds(part * TG, TG)
        pltpu.make_async_remote_copy(
            src_ref=buf.at[0, turns],
            dst_ref=buf.at[s, turns],
            send_sem=send.at[0, part],
            recv_sem=arrive.at[s, part],
            device_id=(source, hour),
            device_id_type=MESH,
        ).wait_recv()

    def hour_of(q):
        return (q + hour + 4 * Z) % HOUR_DEVS

    def choose(r, slot, turns):
        q = z - r + 2 * Z
        for t in turns:
            position = (owner_z[t] + 4 * Z - q) % Z
            lower = position < jnp.maximum(r, 1)
            for i in range(HOURS_DEV):
                rows = pl.ds(i * 16, 16)
                value = lax.select_n(
                    lower, down[Z - 1 - r, t, rows, :], up[r, t, rows, :]
                )
                chosen[t, slot, rows, :] = value.astype(F32)

    def multiply(g, t0, hours):
        start = tuple(
            acc[g, t0 + t, k, c] for t in range(2) for k in range(8) for c in range(2)
        )

        def each(n, sums):
            slot, i = n // HOURS_DEV, n % HOURS_DEV
            h = hours[slot]
            rows = pl.ds(i * 16, 16)
            b = recv[g, h, rows, :].astype(F32)
            b0, b1 = b[:8], b[8:]
            a = [chosen[t0 + t, slot, rows, :] for t in range(2)]
            new = list(sums)
            for k in range(8):
                r0 = pltpu.roll(b0, 8 - k, 0) if k else b0
                r1 = pltpu.roll(b1, 8 - k, 0) if k else b1
                for t in range(2):
                    a0, a1 = a[t][:8], a[t][8:]
                    at = (t * 8 + k) * 2
                    new[at] = new[at] + (a0 * r0 + a1 * r1)
                    new[at + 1] = new[at + 1] + (a1 * r0 - a0 * r1)
            return tuple(new)

        sums = start
        for n in range(2 * HOURS_DEV):
            sums = each(n, sums)
        n = 0
        for t in range(2):
            for k in range(8):
                for c in range(2):
                    acc[g, t0 + t, k, c] = sums[n]
                    n += 1

    def climb(s, part, first=False):
        if not first:
            arrived(up, s, part, up_send, up_recv, below)
        merge(up, s, hour_of(z - s), part * TG, first)
        hop(up, s, part, up_send, up_recv, above).start()

    def descend(s, part, first=False):
        if not first:
            arrived(down, s, part, down_send, down_recv, above)
        merge(down, s, hour_of(z + 1 + s), part * TG, first)
        hop(down, s, part, down_send, down_recv, below).start()

    def step(s):
        for part in range(PARTS):
            climb(s, part)
        for part in range(PARTS):
            descend(s, part)

    def early(s, _):
        wait_pieces(hour_of(z - s))
        for part in range(PARTS):
            climb(s, part)
        wait_pieces(hour_of(z + 1 + s))
        for part in range(PARTS):
            descend(s, part)
        return 0

    def late(s, _):
        step(s)
        low, high = hour_of(z - s), hour_of(z + 1 + s)
        choose(s, 0, range(TURNS))
        choose(Z - 1 - s, 1, range(TURNS))

        def each(n, _):
            multiply(n // 2, (n % 2) * 2, (low, high))
            return 0

        lax.fori_loop(0, GROUPS * 2, each, 0)
        return 0

    wait_pieces(hour_of(z))
    for part in range(PARTS):
        climb(0, part, True)
    wait_pieces(hour_of(z + 1))
    for part in range(PARTS):
        descend(0, part, True)
    others(lambda g: hot_copy(g).start())
    lax.fori_loop(1, 4, early, 0)
    lax.fori_loop(4, Z - 1, late, 0)
    low, high = hour_of(z + 1), hour_of(z)
    others(lambda g: hot_wait(g).wait_recv())

    def deliver(g, part):
        rows = pl.ds(part * TG * 2 * PAIRS, TG * 2 * PAIRS)
        return pltpu.make_async_remote_copy(
            src_ref=picked.at[g, rows],
            dst_ref=halo.at[1 + group, rows],
            send_sem=out_send.at[g, part],
            recv_sem=out_recv.at[1 + group, part],
            device_id=(chan_of(g, z), hour),
            device_id_type=MESH,
        )

    def edge(g, part, to, slot):
        rows = pl.ds(part * TG * 2 * PAIRS, TG * 2 * PAIRS)
        return pltpu.make_async_remote_copy(
            src_ref=picked.at[g, rows],
            dst_ref=halo.at[slot, rows],
            send_sem=edge_send.at[g, part],
            recv_sem=out_recv.at[slot, part],
            device_id=(chan_of(g, z), to),
            device_id_type=MESH,
        )

    to_low = jnp.logical_and(group == 0, hour > 0)
    to_high = jnp.logical_and(group == GROUPS - 1, hour < HOUR_DEVS - 1)

    for part in range(PARTS):
        turns = range(part * TG, part * TG + TG)
        arrived(up, Z - 1, part, up_send, up_recv, below)
        arrived(down, Z - 1, part, down_send, down_recv, above)
        choose(Z - 1, 0, turns)
        choose(0, 1, turns)

        def finish(n, _, part=part, turns=turns):
            g = (group + 1 + n) % GROUPS
            for t in turns[::2]:
                multiply(g, t, (low, high))
            for t in turns:
                table = jnp.concatenate(
                    [acc[g, t, k, c] for k in range(8) for c in range(2)], axis=0
                ).astype(BF16)
                rows = jnp.dot(onehot[g], table, preferred_element_type=F32)
                picked[g, pl.ds(t * 2 * PAIRS, 2 * PAIRS), :] = rows.astype(BF16)

            @pl.when(g != group)
            def _():
                deliver(g, part).start()

            @pl.when(g == group)
            def _():
                rows = pl.ds(part * TG * 2 * PAIRS, TG * 2 * PAIRS)
                halo[1 + group, rows, :] = picked[g, rows, :]

            @pl.when(to_low)
            def _():
                edge(g, part, hour - 1, 5).start()

            @pl.when(to_high)
            def _():
                edge(g, part, hour + 1, 0).start()

            return 0

        lax.fori_loop(0, GROUPS, finish, 0)

    def out_wait(slot, part):
        rows = pl.ds(part * TG * 2 * PAIRS, TG * 2 * PAIRS)
        pltpu.make_async_remote_copy(
            src_ref=picked.at[0, rows],
            dst_ref=halo.at[slot, rows],
            send_sem=out_send.at[0, part],
            recv_sem=out_recv.at[slot, part],
            device_id=(chan, hour),
            device_id_type=MESH,
        ).wait_recv()

    loads[5].wait()
    for part in range(PARTS):
        others(lambda g: out_wait(1 + g, part))

        @pl.when(hour > 0)
        def _():
            out_wait(0, part)

        @pl.when(hour < HOUR_DEVS - 1)
        def _():
            out_wait(5, part)

        rows = pl.ds(part * TG * 2 * PAIRS, TG * 2 * PAIRS)
        for b in range(4):
            total = jnp.dot(halo[b, rows, :], kernel[0, b], preferred_element_type=F32)
            for d in range(1, 3):
                total += jnp.dot(
                    halo[b + d, rows, :], kernel[d, b], preferred_element_type=F32
                )
            for t in range(TG):
                for c in range(2):
                    for p in range(0, PAIRS, 8):
                        at = t * 2 * PAIRS + c * PAIRS + p
                        pair = (part * TG + t) * PAIRS + p
                        merged[pl.ds(pair * 8 + b * 2 + c, 8, stride=8), :] = total[
                            at : at + 8
                        ]
        done = pl.ds(part * TG * PAIRS * 8, TG * PAIRS * 8)
        out[done, :] = merged[done, :].astype(BF16)

    lax.fori_loop(PACED, NB, drain, 0)
    others(lambda g: hot_copy(g).wait_send())
    for part in range(PARTS):
        others(lambda g: deliver(g, part).wait_send())

    def drain_hops(s, _):
        for part in range(PARTS):
            hop(up, s, part, up_send, up_recv, above).wait_send()
            hop(down, s, part, down_send, down_recv, below).wait_send()
        return 0

    lax.fori_loop(0, Z - 1, drain_hops, 0)

    @pl.when(jnp.logical_or(to_low, to_high))
    def _():
        def each(g, _):
            for part in range(PARTS):
                edge(g, part, hour, 0).wait_send()
            return 0

        lax.fori_loop(0, GROUPS, each, 0)


def local(spectra, smooth_kernel, owner_ids, turn_order, source_pick, receiver_pick):
    tiles = spectra.reshape(HOURS_DEV, C_DEV, 2, NB, BAND)
    tiles = tiles.transpose(0, 1, 3, 2, 4).reshape(HOURS_DEV * C_DEV * NB * 2, BAND)
    vmem = pl.BlockSpec(memory_space=pltpu.VMEM)
    hbm = pl.BlockSpec(memory_space=pltpu.HBM)
    rows = TURNS * 2 * PAIRS
    dma = pltpu.SemaphoreType.DMA
    result = pl.pallas_call(
        body,
        out_shape=pltpu.VMEM((rows * 4, BAND), BF16),
        in_specs=[hbm] * 6,
        out_specs=vmem,
        scratch_shapes=[
            pltpu.VMEM((HOURS_DEV * C_DEV * NB * 2, BAND), F32),
            pltpu.VMEM((NB, ROWS, BAND), BF16),
            pltpu.VMEM((GROUPS, HOUR_DEVS, ROWS, BAND), BF16),
            pltpu.VMEM((Z, TURNS, ROWS, BAND), BF16),
            pltpu.VMEM((Z, TURNS, ROWS, BAND), BF16),
            pltpu.VMEM((TURNS, 2, ROWS, BAND), F32),
            pltpu.VMEM((GROUPS, TURNS, 8, 2, 8, BAND), F32),
            pltpu.VMEM((GROUPS, 2 * PAIRS, BAND), BF16),
            pltpu.VMEM((GROUPS, rows, BAND), BF16),
            pltpu.VMEM((6, rows, BAND), BF16),
            pltpu.VMEM((rows * 4, BAND), F32),
            pltpu.VMEM((3, 4, BAND, BAND), BF16),
            pltpu.SMEM((TURNS,), jnp.int32),
            pltpu.SMEM((TURNS,), jnp.int32),
            pltpu.VMEM((1, PAIRS), jnp.int32),
            pltpu.VMEM((1, PAIRS), jnp.int32),
            dma((6,)),
            dma((NB,)),
            dma((GROUPS, HOUR_DEVS)),
            dma((Z, PARTS)),
            dma((Z, PARTS)),
            dma((Z, PARTS)),
            dma((Z, PARTS)),
            dma((GROUPS,)),
            dma((GROUPS,)),
            dma((GROUPS, PARTS)),
            dma((6, PARTS)),
            dma((GROUPS, PARTS)),
        ],
        compiler_params=pltpu.CompilerParams(
            collective_id=0, has_side_effects=True, vmem_limit_bytes=63 * 1024 * 1024
        ),
    )(
        tiles,
        smooth_kernel,
        owner_ids,
        turn_order,
        source_pick.reshape(1, PAIRS),
        receiver_pick.reshape(1, PAIRS),
    )
    result = result.reshape(TURNS, PAIRS, 4, 2, BAND).transpose(0, 1, 3, 2, 4)
    return result.reshape(TURNS, PAIRS, 2, 4 * BAND)


def solution(mesh):
    return jax.shard_map(
        local,
        mesh=mesh,
        in_specs=(
            P("hour", "chan", None, None),
            P(None, "hour", None, None),
            P(),
            P(),
            P("chan"),
            P("chan"),
        ),
        out_specs=P(None, "chan", None, "hour"),
        check_vma=False,
    )
```

```python
import jax
import jax.numpy as jnp
from jax import lax
from jax.experimental import pallas as pl
from jax.experimental.pallas import tpu as pltpu
from jax.sharding import PartitionSpec as P

MESH = pl.DeviceIdType.MESH

BAND = 128
TURNS = 4
C_DEV = 8
PAIRS = 32
HOUR_DEVS = 8
HOURS_DEV = 6
Z = 8
GROUPS = 4
ROWS = HOURS_DEV * 16
TG = 2
PARTS = TURNS // TG
FIRST = 24
NB = 32
BF16 = jnp.bfloat16
F32 = jnp.float32


def body(
    spectra, kernel_hbm, owners_hbm, order_hbm, source_hbm, receiver_hbm, out,
    raw, staged, recv, up, down, chosen, acc, onehot, picked, halo, merged,
    kernel, owner_ids, turn_order, source_pick, receiver_pick, load_sem,
    a2a_send, a2a_recv, up_send, up_recv, down_send, down_recv,
    hot_send, hot_recv, out_send, out_recv, edge_send,
):
    chan = lax.axis_index("chan")
    hour = lax.axis_index("hour")
    core = chan % 2
    z = (chan // 2) % Z
    y_hi = chan // (2 * Z)
    group = y_hi * 2 + core

    def chan_of(g, level):
        return ((g // 2) * Z + level) * 2 + g % 2

    loads = [
        pltpu.make_async_copy(a, b, load_sem.at[n])
        for n, (a, b) in enumerate(
            [
                (spectra, raw),
                (owners_hbm, owner_ids),
                (order_hbm, turn_order),
                (source_hbm, source_pick),
                (receiver_hbm, receiver_pick),
                (kernel_hbm, kernel),
            ]
        )
    ]
    for load in loads:
        load.start()

    barrier = pltpu.get_barrier_semaphore()

    def greet(n, _):
        g, h = n // HOUR_DEVS, n % HOUR_DEVS

        @pl.when(jnp.logical_or(g != group, h != hour))
        def _():
            pl.semaphore_signal(
                barrier, inc=1, device_id=(chan_of(g, z), h), device_id_type=MESH
            )

        return 0

    above = chan_of(group, (z + 1) % Z)
    below = chan_of(group, (z + Z - 1) % Z)
    lax.fori_loop(0, NB, greet, 0)
    pl.semaphore_signal(barrier, inc=1, device_id=(above, hour), device_id_type=MESH)
    pl.semaphore_signal(barrier, inc=1, device_id=(below, hour), device_id_type=MESH)

    for load in loads[3:5]:
        load.wait()

    src = source_pick[...]
    rec = receiver_pick[...]
    code = (((rec - src) & 7) * 16 + src).astype(F32)
    row = lax.broadcasted_iota(jnp.int32, (PAIRS, PAIRS), 0)
    col = lax.broadcasted_iota(jnp.int32, (PAIRS, PAIRS), 1)
    spread = jnp.where(row == col, jnp.broadcast_to(code, (PAIRS, PAIRS)), 0.0)
    code_col = jnp.sum(spread, axis=1, keepdims=True)
    lane = lax.broadcasted_iota(jnp.int32, (PAIRS, BAND), 1).astype(F32)
    for c in range(2):
        hot = jnp.where(lane == code_col + 8.0 * c, 1.0, 0.0)
        onehot[group, pl.ds(c * PAIRS, PAIRS), :] = hot.astype(BF16)

    acc[...] = jnp.zeros_like(acc)

    @pl.when(hour == 0)
    def _():
        halo[0] = jnp.zeros((2 * TURNS * PAIRS, BAND), BF16)

    @pl.when(hour == HOUR_DEVS - 1)
    def _():
        halo[5] = jnp.zeros((2 * TURNS * PAIRS, BAND), BF16)

    for load in loads[:3]:
        load.wait()
    pl.semaphore_wait(barrier, NB + 1)

    def a2a(g, h):
        band = h * GROUPS + g
        return pltpu.make_async_remote_copy(
            src_ref=staged.at[band],
            dst_ref=recv.at[group, hour],
            send_sem=a2a_send.at[band],
            recv_sem=a2a_recv.at[group, hour],
            device_id=(chan_of(g, z), h),
            device_id_type=MESH,
        )

    def shift_of(q):
        q = (q + 2 * Z) % Z
        return q // 4, q % 4

    def hour_of(q):
        far, along = shift_of(q)
        return (hour // 4 + far) % 2 * 4 + (hour + along) % 4

    def hour_for(q):
        far, along = shift_of(q)
        return (hour // 4 + far) % 2 * 4 + (hour + 4 - along) % 4

    def target(n):
        k = n // GROUPS
        g = (group + n) % GROUPS
        step = (k + 1) // 2
        shift = jnp.where(k % 2 == 1, step, 2 * Z - step)
        return g, hour_for(z + shift)

    def scatter(n, _):
        g, h = target(n)
        band = h * GROUPS + g
        mine = jnp.logical_and(g == group, h == hour)
        for i in range(HOURS_DEV):
            parts = [
                raw[pl.ds(i * 512 + band * 2 + p, 8, stride=64), :] for p in range(2)
            ]
            staged[band, pl.ds(i * 16, 16), :] = jnp.concatenate(parts, 0).astype(BF16)

        @pl.when(jnp.logical_not(mine))
        def _():
            a2a(g, h).start()

        @pl.when(mine)
        def _():
            recv[group, hour] = staged[band]

        return 0

    def drain(n, _):
        g, h = target(n)

        @pl.when(jnp.logical_or(g != group, h != hour))
        def _():
            a2a(g, h).wait_send()

        return 0

    lax.fori_loop(0, FIRST, scatter, 0)

    def hot_copy(g):
        return pltpu.make_async_remote_copy(
            src_ref=onehot.at[group],
            dst_ref=onehot.at[group],
            send_sem=hot_send.at[g],
            recv_sem=hot_recv.at[group],
            device_id=(chan_of(g, z), hour),
            device_id_type=MESH,
        )

    def hot_wait(g):
        return pltpu.make_async_remote_copy(
            src_ref=onehot.at[group],
            dst_ref=onehot.at[g],
            send_sem=hot_send.at[g],
            recv_sem=hot_recv.at[g],
            device_id=(chan_of(g, z), hour),
            device_id_type=MESH,
        )

    def others(fn):
        def each(n, _):
            fn((group + n) % GROUPS)
            return 0

        lax.fori_loop(1, GROUPS, each, 0)


    owners = [owner_ids[turn_order[t]] for t in range(TURNS)]
    owner_z = [(o // 2) % Z for o in owners]
    owner_g = [(o // (2 * Z)) * 2 + o % 2 for o in owners]

    def wait_pieces(h):
        def each(g, _):
            @pl.when(jnp.logical_or(g != group, h != hour))
            def _():
                pltpu.make_async_remote_copy(
                    src_ref=staged.at[0],
                    dst_ref=recv.at[g, h],
                    send_sem=a2a_send.at[0],
                    recv_sem=a2a_recv.at[g, h],
                    device_id=(chan_of(g, z), h),
                    device_id_type=MESH,
                ).wait_recv()

            return 0

        lax.fori_loop(0, GROUPS, each, 0)

    def merge(buf, s, h, t0, first):
        for i in range(HOURS_DEV):
            rows = pl.ds(i * 16, 16)
            held = [recv[g, h, rows, :] for g in range(GROUPS)]
            for t in range(t0, t0 + TG):
                mine = held[0]
                for g in range(1, GROUPS):
                    mine = lax.select_n(owner_g[t] == g, mine, held[g])
                if not first:
                    mine = lax.select_n(owner_z[t] == z, buf[s, t, rows, :], mine)
                buf[s, t, rows, :] = mine

    def hop(buf, s, part, send, arrive, target):
        turns = pl.ds(part * TG, TG)
        return pltpu.make_async_remote_copy(
            src_ref=buf.at[s, turns],
            dst_ref=buf.at[s + 1, turns],
            send_sem=send.at[s, part],
            recv_sem=arrive.at[s + 1, part],
            device_id=(target, hour),
            device_id_type=MESH,
        )

    def arrived(buf, s, part, send, arrive, source):
        turns = pl.ds(part * TG, TG)
        pltpu.make_async_remote_copy(
            src_ref=buf.at[0, turns],
            dst_ref=buf.at[s, turns],
            send_sem=send.at[0, part],
            recv_sem=arrive.at[s, part],
            device_id=(source, hour),
            device_id_type=MESH,
        ).wait_recv()

    def choose(r, slot, turns):
        q = z - r + 2 * Z
        for t in turns:
            position = (owner_z[t] + 4 * Z - q) % Z
            lower = position < jnp.maximum(r, 1)
            for i in range(HOURS_DEV):
                rows = pl.ds(i * 16, 16)
                value = lax.select_n(
                    lower, down[Z - 1 - r, t, rows, :], up[r, t, rows, :]
                )
                chosen[t, slot, rows, :] = value.astype(F32)

    def multiply(g, t0, hours):
        for k0 in range(0, 8, 4):
            span = range(k0, k0 + 4)
            sums = [acc[g, t0 + t, k, c] for t in range(2) for k in span for c in range(3)]
            for slot in range(2):
                for i in range(HOURS_DEV):
                    rows = pl.ds(i * 16, 16)
                    b = recv[g, hours[slot], rows, :].astype(F32)
                    b0, b1 = b[:8], b[8:]
                    a = [chosen[t0 + t, slot, rows, :] for t in range(2)]
                    a = [(x[:8], x[8:], x[:8] + x[8:]) for x in a]
                    for k in span:
                        r0 = pltpu.roll(b0, 8 - k, 0) if k else b0
                        r1 = pltpu.roll(b1, 8 - k, 0) if k else b1
                        rd = r0 - r1
                        for t in range(2):
                            at = (t * 4 + k - k0) * 3
                            sums[at] = sums[at] + a[t][0] * r0
                            sums[at + 1] = sums[at + 1] + a[t][1] * r1
                            sums[at + 2] = sums[at + 2] + a[t][2] * rd
            n = 0
            for t in range(2):
                for k in span:
                    for c in range(3):
                        acc[g, t0 + t, k, c] = sums[n]
                        n += 1

    def table_of(g, t):
        parts = []
        for k in range(8):
            real, imag, cross = (acc[g, t, k, c] for c in range(3))
            parts += [real + imag, cross - real + imag]
        return jnp.concatenate(parts, axis=0).astype(BF16)

    def climb(s, part, first=False):
        if not first:
            arrived(up, s, part, up_send, up_recv, below)
        merge(up, s, hour_of(z - s), part * TG, first)
        hop(up, s, part, up_send, up_recv, above).start()

    def descend(s, part, first=False):
        if not first:
            arrived(down, s, part, down_send, down_recv, above)
        merge(down, s, hour_of(z + 1 + s), part * TG, first)
        hop(down, s, part, down_send, down_recv, below).start()

    def step(s):
        for part in range(PARTS):
            climb(s, part)
        for part in range(PARTS):
            descend(s, part)

    def early(s, _):
        wait_pieces(hour_of(z - s))
        for part in range(PARTS):
            climb(s, part)
        wait_pieces(hour_of(z + 1 + s))
        for part in range(PARTS):
            descend(s, part)
        lax.fori_loop(s * 8 - 8, s * 8, drain, 0)
        return 0

    def drain_hops(s, _):
        for part in range(PARTS):
            hop(up, s, part, up_send, up_recv, above).wait_send()
            hop(down, s, part, down_send, down_recv, below).wait_send()
        return 0

    def late(s, _):
        step(s)
        low, high = hour_of(z - s), hour_of(z + 1 + s)
        choose(s, 0, range(TURNS))
        choose(Z - 1 - s, 1, range(TURNS))

        def each(n, _):
            multiply(n // 2, (n % 2) * 2, (low, high))
            return 0

        lax.fori_loop(0, GROUPS * 2, each, 0)
        drain_hops(s - 2, 0)
        return 0

    wait_pieces(hour_of(z))
    for part in range(PARTS):
        climb(0, part, True)
    wait_pieces(hour_of(z + 1))
    for part in range(PARTS):
        descend(0, part, True)
    lax.fori_loop(FIRST, NB, scatter, 0)
    others(lambda g: hot_copy(g).start())
    lax.fori_loop(1, 4, early, 0)
    lax.fori_loop(NB * 3 // 4, NB, drain, 0)
    others(lambda g: hot_copy(g).wait_send())
    lax.fori_loop(0, 2, drain_hops, 0)
    lax.fori_loop(4, Z - 1, late, 0)
    low, high = hour_of(z + 1), hour_of(z)
    others(lambda g: hot_wait(g).wait_recv())

    def deliver(g, part):
        rows = pl.ds(part * TG * 2 * PAIRS, TG * 2 * PAIRS)
        return pltpu.make_async_remote_copy(
            src_ref=picked.at[g, rows],
            dst_ref=halo.at[1 + group, rows],
            send_sem=out_send.at[g, part],
            recv_sem=out_recv.at[1 + group, part],
            device_id=(chan_of(g, z), hour),
            device_id_type=MESH,
        )

    def edge(g, part, to, slot):
        rows = pl.ds(part * TG * 2 * PAIRS, TG * 2 * PAIRS)
        return pltpu.make_async_remote_copy(
            src_ref=picked.at[g, rows],
            dst_ref=halo.at[slot, rows],
            send_sem=edge_send.at[g, part],
            recv_sem=out_recv.at[slot, part],
            device_id=(chan_of(g, z), to),
            device_id_type=MESH,
        )

    to_low = jnp.logical_and(group == 0, hour > 0)
    to_high = jnp.logical_and(group == GROUPS - 1, hour < HOUR_DEVS - 1)

    for part in range(PARTS):
        turns = range(part * TG, part * TG + TG)
        arrived(up, Z - 1, part, up_send, up_recv, below)
        arrived(down, Z - 1, part, down_send, down_recv, above)
        choose(Z - 1, 0, turns)
        choose(0, 1, turns)

        def finish(n, _, part=part, turns=turns):
            g = (group + 1 + n) % GROUPS
            for t in turns[::2]:
                multiply(g, t, (low, high))
            table = jnp.concatenate(
                [
                    table_of(g, t)
                    for t in turns
                ],
                axis=1,
            )
            rows = jnp.dot(onehot[g], table, preferred_element_type=F32).astype(BF16)
            for n2, t in enumerate(turns):
                picked[g, pl.ds(t * 2 * PAIRS, 2 * PAIRS), :] = rows[
                    :, n2 * BAND : (n2 + 1) * BAND
                ]

            @pl.when(g != group)
            def _():
                deliver(g, part).start()

            @pl.when(g == group)
            def _():
                rows = pl.ds(part * TG * 2 * PAIRS, TG * 2 * PAIRS)
                halo[1 + group, rows, :] = picked[g, rows, :]

            @pl.when(to_low)
            def _():
                edge(g, part, hour - 1, 5).start()

            @pl.when(to_high)
            def _():
                edge(g, part, hour + 1, 0).start()

            return 0

        lax.fori_loop(0, GROUPS, finish, 0)

    def out_wait(slot, part):
        rows = pl.ds(part * TG * 2 * PAIRS, TG * 2 * PAIRS)
        pltpu.make_async_remote_copy(
            src_ref=picked.at[0, rows],
            dst_ref=halo.at[slot, rows],
            send_sem=out_send.at[0, part],
            recv_sem=out_recv.at[slot, part],
            device_id=(chan, hour),
            device_id_type=MESH,
        ).wait_recv()

    loads[5].wait()
    for part in range(PARTS):
        others(lambda g: out_wait(1 + g, part))

        @pl.when(hour > 0)
        def _():
            out_wait(0, part)

        @pl.when(hour < HOUR_DEVS - 1)
        def _():
            out_wait(5, part)

        rows = pl.ds(part * TG * 2 * PAIRS, TG * 2 * PAIRS)
        for b in range(4):
            total = jnp.dot(halo[b, rows, :], kernel[0, b], preferred_element_type=F32)
            for d in range(1, 3):
                total += jnp.dot(
                    halo[b + d, rows, :], kernel[d, b], preferred_element_type=F32
                )
            for t in range(TG):
                for c in range(2):
                    for p in range(0, PAIRS, 8):
                        at = t * 2 * PAIRS + c * PAIRS + p
                        pair = (part * TG + t) * PAIRS + p
                        merged[pl.ds(pair * 8 + b * 2 + c, 8, stride=8), :] = total[
                            at : at + 8
                        ]
        done = pl.ds(part * TG * PAIRS * 8, TG * PAIRS * 8)
        out[done, :] = merged[done, :].astype(BF16)

    for part in range(PARTS):
        others(lambda g: deliver(g, part).wait_send())

    lax.fori_loop(5, Z - 1, drain_hops, 0)

    @pl.when(jnp.logical_or(to_low, to_high))
    def _():
        def each(g, _):
            for part in range(PARTS):
                edge(g, part, hour, 0).wait_send()
            return 0

        lax.fori_loop(0, GROUPS, each, 0)


def local(spectra, smooth_kernel, owner_ids, turn_order, source_pick, receiver_pick):
    tiles = spectra.reshape(HOURS_DEV, C_DEV, 2, NB, BAND)
    tiles = tiles.transpose(0, 1, 3, 2, 4).reshape(HOURS_DEV * C_DEV * NB * 2, BAND)
    vmem = pl.BlockSpec(memory_space=pltpu.VMEM)
    hbm = pl.BlockSpec(memory_space=pltpu.HBM)
    rows = TURNS * 2 * PAIRS
    dma = pltpu.SemaphoreType.DMA
    result = pl.pallas_call(
        body,
        out_shape=pltpu.VMEM((rows * 4, BAND), BF16),
        in_specs=[hbm] * 6,
        out_specs=vmem,
        scratch_shapes=[
            pltpu.VMEM((HOURS_DEV * C_DEV * NB * 2, BAND), F32),
            pltpu.VMEM((NB, ROWS, BAND), BF16),
            pltpu.VMEM((GROUPS, HOUR_DEVS, ROWS, BAND), BF16),
            pltpu.VMEM((Z, TURNS, ROWS, BAND), BF16),
            pltpu.VMEM((Z, TURNS, ROWS, BAND), BF16),
            pltpu.VMEM((TURNS, 2, ROWS, BAND), F32),
            pltpu.VMEM((GROUPS, TURNS, 8, 3, 8, BAND), F32),
            pltpu.VMEM((GROUPS, 2 * PAIRS, BAND), BF16),
            pltpu.VMEM((GROUPS, rows, BAND), BF16),
            pltpu.VMEM((6, rows, BAND), BF16),
            pltpu.VMEM((rows * 4, BAND), F32),
            pltpu.VMEM((3, 4, BAND, BAND), BF16),
            pltpu.SMEM((TURNS,), jnp.int32),
            pltpu.SMEM((TURNS,), jnp.int32),
            pltpu.VMEM((1, PAIRS), jnp.int32),
            pltpu.VMEM((1, PAIRS), jnp.int32),
            dma((6,)),
            dma((NB,)),
            dma((GROUPS, HOUR_DEVS)),
            dma((Z, PARTS)),
            dma((Z, PARTS)),
            dma((Z, PARTS)),
            dma((Z, PARTS)),
            dma((GROUPS,)),
            dma((GROUPS,)),
            dma((GROUPS, PARTS)),
            dma((6, PARTS)),
            dma((GROUPS, PARTS)),
        ],
        compiler_params=pltpu.CompilerParams(
            collective_id=0, has_side_effects=True, vmem_limit_bytes=63 * 1024 * 1024
        ),
    )(
        tiles,
        smooth_kernel,
        owner_ids,
        turn_order,
        source_pick.reshape(1, PAIRS),
        receiver_pick.reshape(1, PAIRS),
    )
    result = result.reshape(TURNS, PAIRS, 4, 2, BAND).transpose(0, 1, 3, 2, 4)
    return result.reshape(TURNS, PAIRS, 2, 4 * BAND)


def solution(mesh):
    return jax.shard_map(
        local,
        mesh=mesh,
        in_specs=(
            P("hour", "chan", None, None),
            P(None, "hour", None, None),
            P(),
            P(),
            P("chan"),
            P("chan"),
        ),
        out_specs=P(None, "chan", None, "hour"),
        check_vma=False,
    )
```

```python
import jax
import jax.numpy as jnp
from jax import lax
from jax.experimental import pallas as pl
from jax.experimental.pallas import tpu as pltpu
from jax.sharding import PartitionSpec as P

MESH = pl.DeviceIdType.MESH

BAND = 128
TURNS = 4
C_DEV = 8
PAIRS = 32
HOUR_DEVS = 8
HOURS_DEV = 6
Z = 8
GROUPS = 4
ROWS = HOURS_DEV * 16
TG = 2
PARTS = TURNS // TG
FIRST = 24
NB = 32
TILE_ROWS = HOURS_DEV * C_DEV * NB * 2
BF16 = jnp.bfloat16
F32 = jnp.float32


def body(
    spectra, kernel_hbm, owners_hbm, order_hbm, source_hbm, receiver_hbm, out,
    raw, staged, recv, up, down, chosen, acc, onehot, picked, halo, merged,
    kernel, owner_ids, turn_order, source_pick, receiver_pick, load_sem,
    a2a_send, a2a_recv, up_send, up_recv, down_send, down_recv,
    hot_send, hot_recv, out_send, out_recv, edge_send,
):
    chan = lax.axis_index("chan")
    hour = lax.axis_index("hour")
    core = chan % 2
    z = (chan // 2) % Z
    y_hi = chan // (2 * Z)
    group = y_hi * 2 + core

    def chan_of(g, level):
        return ((g // 2) * Z + level) * 2 + g % 2

    loads = [
        pltpu.make_async_copy(a, b, load_sem.at[n])
        for n, (a, b) in enumerate(
            [
                (spectra, raw.at[pl.ds(0, TILE_ROWS)]),
                (owners_hbm, owner_ids),
                (order_hbm, turn_order),
                (source_hbm, source_pick),
                (receiver_hbm, receiver_pick),
                (kernel_hbm, kernel),
            ]
        )
    ]
    for load in loads:
        load.start()

    barrier = pltpu.get_barrier_semaphore()

    def greet(n, _):
        g, h = n // HOUR_DEVS, n % HOUR_DEVS

        @pl.when(jnp.logical_or(g != group, h != hour))
        def _():
            pl.semaphore_signal(
                barrier, inc=1, device_id=(chan_of(g, z), h), device_id_type=MESH
            )

        return 0

    above = chan_of(group, (z + 1) % Z)
    below = chan_of(group, (z + Z - 1) % Z)
    lax.fori_loop(0, NB, greet, 0)
    pl.semaphore_signal(barrier, inc=1, device_id=(above, hour), device_id_type=MESH)
    pl.semaphore_signal(barrier, inc=1, device_id=(below, hour), device_id_type=MESH)

    for load in loads[3:5]:
        load.wait()

    src = source_pick[...]
    rec = receiver_pick[...]
    code = (((rec - src) & 7) * 16 + src).astype(F32)
    row = lax.broadcasted_iota(jnp.int32, (PAIRS, PAIRS), 0)
    col = lax.broadcasted_iota(jnp.int32, (PAIRS, PAIRS), 1)
    spread = jnp.where(row == col, jnp.broadcast_to(code, (PAIRS, PAIRS)), 0.0)
    code_col = jnp.sum(spread, axis=1, keepdims=True)
    lane = lax.broadcasted_iota(jnp.int32, (PAIRS, BAND), 1).astype(F32)
    for c in range(2):
        hot = jnp.where(lane == code_col + 8.0 * c, 1.0, 0.0)
        onehot[group, pl.ds(c * PAIRS, PAIRS), :] = hot.astype(BF16)

    acc[...] = jnp.zeros_like(acc)

    @pl.when(hour == 0)
    def _():
        halo[0] = jnp.zeros((2 * TURNS * PAIRS, BAND), BF16)

    @pl.when(hour == HOUR_DEVS - 1)
    def _():
        halo[5] = jnp.zeros((2 * TURNS * PAIRS, BAND), BF16)

    for load in loads[:3]:
        load.wait()
    pl.semaphore_wait(barrier, NB + 1)

    def a2a(g, h):
        band = h * GROUPS + g
        return pltpu.make_async_remote_copy(
            src_ref=staged.at[band],
            dst_ref=recv.at[group, hour],
            send_sem=a2a_send.at[band],
            recv_sem=a2a_recv.at[group, hour],
            device_id=(chan_of(g, z), h),
            device_id_type=MESH,
        )

    def shift_of(q):
        q = (q + 2 * Z) % Z
        return q // 4, q % 4

    def hour_of(q):
        far, along = shift_of(q)
        return (hour // 4 + far) % 2 * 4 + (hour + along) % 4

    def hour_for(q):
        far, along = shift_of(q)
        return (hour // 4 + far) % 2 * 4 + (hour + 4 - along) % 4

    def target(n):
        k = n // GROUPS
        g = (group + n) % GROUPS
        step = (k + 1) // 2
        shift = jnp.where(k % 2 == 1, step, 2 * Z - step)
        return g, hour_for(z + shift)

    def scatter(n, _):
        g, h = target(n)
        band = h * GROUPS + g
        mine = jnp.logical_and(g == group, h == hour)
        for i in range(HOURS_DEV):
            parts = [
                raw[pl.ds(i * 512 + band * 2 + p, 8, stride=64), :] for p in range(2)
            ]
            staged[band, pl.ds(i * 16, 16), :] = jnp.concatenate(parts, 0).astype(BF16)

        @pl.when(jnp.logical_not(mine))
        def _():
            a2a(g, h).start()

        @pl.when(mine)
        def _():
            recv[group, hour] = staged[band]

        return 0

    def drain(n, _):
        g, h = target(n)

        @pl.when(jnp.logical_or(g != group, h != hour))
        def _():
            a2a(g, h).wait_send()

        return 0

    lax.fori_loop(0, FIRST, scatter, 0)

    def hot_copy(g):
        return pltpu.make_async_remote_copy(
            src_ref=onehot.at[group],
            dst_ref=onehot.at[group],
            send_sem=hot_send.at[g],
            recv_sem=hot_recv.at[group],
            device_id=(chan_of(g, z), hour),
            device_id_type=MESH,
        )

    def hot_wait(g):
        return pltpu.make_async_remote_copy(
            src_ref=onehot.at[group],
            dst_ref=onehot.at[g],
            send_sem=hot_send.at[g],
            recv_sem=hot_recv.at[g],
            device_id=(chan_of(g, z), hour),
            device_id_type=MESH,
        )

    def others(fn):
        def each(n, _):
            fn((group + n) % GROUPS)
            return 0

        lax.fori_loop(1, GROUPS, each, 0)


    owners = [owner_ids[turn_order[t]] for t in range(TURNS)]
    owner_z = [(o // 2) % Z for o in owners]
    owner_g = [(o // (2 * Z)) * 2 + o % 2 for o in owners]

    def wait_pieces(h):
        def each(g, _):
            @pl.when(jnp.logical_or(g != group, h != hour))
            def _():
                pltpu.make_async_remote_copy(
                    src_ref=staged.at[0],
                    dst_ref=recv.at[g, h],
                    send_sem=a2a_send.at[0],
                    recv_sem=a2a_recv.at[g, h],
                    device_id=(chan_of(g, z), h),
                    device_id_type=MESH,
                ).wait_recv()

            return 0

        lax.fori_loop(0, GROUPS, each, 0)

    def merge(buf, s, h, t0, first):
        for i in range(HOURS_DEV):
            rows = pl.ds(i * 16, 16)
            held = [recv[g, h, rows, :] for g in range(GROUPS)]
            for t in range(t0, t0 + TG):
                mine = held[0]
                for g in range(1, GROUPS):
                    mine = lax.select_n(owner_g[t] == g, mine, held[g])
                if not first:
                    mine = lax.select_n(owner_z[t] == z, buf[s, t, rows, :], mine)
                buf[s, t, rows, :] = mine

    def hop(buf, s, part, send, arrive, target):
        turns = pl.ds(part * TG, TG)
        return pltpu.make_async_remote_copy(
            src_ref=buf.at[s, turns],
            dst_ref=buf.at[s + 1, turns],
            send_sem=send.at[s, part],
            recv_sem=arrive.at[s + 1, part],
            device_id=(target, hour),
            device_id_type=MESH,
        )

    def arrived(buf, s, part, send, arrive, source):
        turns = pl.ds(part * TG, TG)
        pltpu.make_async_remote_copy(
            src_ref=buf.at[0, turns],
            dst_ref=buf.at[s, turns],
            send_sem=send.at[0, part],
            recv_sem=arrive.at[s, part],
            device_id=(source, hour),
            device_id_type=MESH,
        ).wait_recv()

    def choose(r, slot, turns):
        q = z - r + 2 * Z
        for t in turns:
            position = (owner_z[t] + 4 * Z - q) % Z
            lower = position < jnp.maximum(r, 1)
            for i in range(HOURS_DEV):
                rows = pl.ds(i * 16, 16)
                value = lax.select_n(
                    lower, down[Z - 1 - r, t, rows, :], up[r, t, rows, :]
                )
                chosen[t, slot, rows, :] = value.astype(F32)

    def multiply(g, t0, hours):
        for k0 in range(0, 8, 4):
            span = range(k0, k0 + 4)
            sums = [acc[g, t0 + t, k, c] for t in range(2) for k in span for c in range(3)]
            for slot in range(2):
                for i in range(HOURS_DEV):
                    rows = pl.ds(i * 16, 16)
                    b = recv[g, hours[slot], rows, :].astype(F32)
                    b0, b1 = b[:8], b[8:]
                    a = [chosen[t0 + t, slot, rows, :] for t in range(2)]
                    a = [(x[:8], x[8:], x[:8] + x[8:]) for x in a]
                    for k in span:
                        r0 = pltpu.roll(b0, 8 - k, 0) if k else b0
                        r1 = pltpu.roll(b1, 8 - k, 0) if k else b1
                        rd = r0 - r1
                        for t in range(2):
                            at = (t * 4 + k - k0) * 3
                            sums[at] = sums[at] + a[t][0] * r0
                            sums[at + 1] = sums[at + 1] + a[t][1] * r1
                            sums[at + 2] = sums[at + 2] + a[t][2] * rd
            n = 0
            for t in range(2):
                for k in span:
                    for c in range(3):
                        acc[g, t0 + t, k, c] = sums[n]
                        n += 1

    def table_of(g, t):
        parts = []
        for k in range(8):
            real, imag, cross = (acc[g, t, k, c] for c in range(3))
            parts += [real + imag, cross - real + imag]
        return jnp.concatenate(parts, axis=0).astype(BF16)

    def climb(s, part, first=False):
        if not first:
            arrived(up, s, part, up_send, up_recv, below)
        merge(up, s, hour_of(z - s), part * TG, first)
        hop(up, s, part, up_send, up_recv, above).start()

    def descend(s, part, first=False):
        if not first:
            arrived(down, s, part, down_send, down_recv, above)
        merge(down, s, hour_of(z + 1 + s), part * TG, first)
        hop(down, s, part, down_send, down_recv, below).start()

    def step(s):
        for part in range(PARTS):
            climb(s, part)
        for part in range(PARTS):
            descend(s, part)

    def early(s, _):
        wait_pieces(hour_of(z - s))
        for part in range(PARTS):
            climb(s, part)
        wait_pieces(hour_of(z + 1 + s))
        for part in range(PARTS):
            descend(s, part)
        lax.fori_loop(s * 8 - 8, s * 8, drain, 0)
        return 0

    def drain_hops(s, _):
        for part in range(PARTS):
            hop(up, s, part, up_send, up_recv, above).wait_send()
            hop(down, s, part, down_send, down_recv, below).wait_send()
        return 0

    def late(s, _):
        step(s)
        low, high = hour_of(z - s), hour_of(z + 1 + s)
        choose(s, 0, range(TURNS))
        choose(Z - 1 - s, 1, range(TURNS))

        def each(n, _):
            multiply(n // 2, (n % 2) * 2, (low, high))
            return 0

        lax.fori_loop(0, GROUPS * 2, each, 0)
        drain_hops(s - 2, 0)
        return 0

    wait_pieces(hour_of(z))
    for part in range(PARTS):
        climb(0, part, True)
    wait_pieces(hour_of(z + 1))
    for part in range(PARTS):
        descend(0, part, True)
    lax.fori_loop(FIRST, NB, scatter, 0)
    others(lambda g: hot_copy(g).start())
    lax.fori_loop(1, 4, early, 0)
    lax.fori_loop(NB * 3 // 4, NB, drain, 0)
    others(lambda g: hot_copy(g).wait_send())
    lax.fori_loop(0, 2, drain_hops, 0)
    lax.fori_loop(4, Z - 1, late, 0)
    low, high = hour_of(z + 1), hour_of(z)
    others(lambda g: hot_wait(g).wait_recv())

    def deliver(g, part):
        rows = pl.ds(part * TG * 2 * PAIRS, TG * 2 * PAIRS)
        return pltpu.make_async_remote_copy(
            src_ref=picked.at[g, rows],
            dst_ref=halo.at[1 + group, rows],
            send_sem=out_send.at[g, part],
            recv_sem=out_recv.at[1 + group, part],
            device_id=(chan_of(g, z), hour),
            device_id_type=MESH,
        )

    def edge(g, part, to, slot):
        rows = pl.ds(part * TG * 2 * PAIRS, TG * 2 * PAIRS)
        return pltpu.make_async_remote_copy(
            src_ref=picked.at[g, rows],
            dst_ref=halo.at[slot, rows],
            send_sem=edge_send.at[g, part],
            recv_sem=out_recv.at[slot, part],
            device_id=(chan_of(g, z), to),
            device_id_type=MESH,
        )

    to_low = jnp.logical_and(group == 0, hour > 0)
    to_high = jnp.logical_and(group == GROUPS - 1, hour < HOUR_DEVS - 1)

    for part in range(PARTS):
        turns = range(part * TG, part * TG + TG)
        arrived(up, Z - 1, part, up_send, up_recv, below)
        arrived(down, Z - 1, part, down_send, down_recv, above)
        choose(Z - 1, 0, turns)
        choose(0, 1, turns)

        def finish(n, _, part=part, turns=turns):
            g = (group + 1 + n) % GROUPS
            for t in turns[::2]:
                multiply(g, t, (low, high))
            table = jnp.concatenate(
                [
                    table_of(g, t)
                    for t in turns
                ],
                axis=1,
            )
            rows = jnp.dot(onehot[g], table, preferred_element_type=F32).astype(BF16)
            for n2, t in enumerate(turns):
                picked[g, pl.ds(t * 2 * PAIRS, 2 * PAIRS), :] = rows[
                    :, n2 * BAND : (n2 + 1) * BAND
                ]

            @pl.when(g != group)
            def _():
                deliver(g, part).start()

            @pl.when(g == group)
            def _():
                rows = pl.ds(part * TG * 2 * PAIRS, TG * 2 * PAIRS)
                halo[1 + group, rows, :] = picked[g, rows, :]

            @pl.when(to_low)
            def _():
                edge(g, part, hour - 1, 5).start()

            @pl.when(to_high)
            def _():
                edge(g, part, hour + 1, 0).start()

            return 0

        lax.fori_loop(0, GROUPS, finish, 0)

    def out_wait(slot, part):
        rows = pl.ds(part * TG * 2 * PAIRS, TG * 2 * PAIRS)
        pltpu.make_async_remote_copy(
            src_ref=picked.at[0, rows],
            dst_ref=halo.at[slot, rows],
            send_sem=out_send.at[0, part],
            recv_sem=out_recv.at[slot, part],
            device_id=(chan, hour),
            device_id_type=MESH,
        ).wait_recv()

    loads[5].wait()
    for part in range(PARTS):
        others(lambda g: out_wait(1 + g, part))

        @pl.when(hour > 0)
        def _():
            out_wait(0, part)

        @pl.when(hour < HOUR_DEVS - 1)
        def _():
            out_wait(5, part)

        rows = pl.ds(part * TG * 2 * PAIRS, TG * 2 * PAIRS)
        for b in range(4):
            total = jnp.dot(halo[b, rows, :], kernel[0, b], preferred_element_type=F32)
            for d in range(1, 3):
                total += jnp.dot(
                    halo[b + d, rows, :], kernel[d, b], preferred_element_type=F32
                )
            for t in range(TG):
                for c in range(2):
                    for p in range(0, PAIRS, 8):
                        at = t * 2 * PAIRS + c * PAIRS + p
                        pair = (part * TG + t) * PAIRS + p
                        merged[pl.ds(pair * 8 + b * 2 + c, 8, stride=8), :] = total[
                            at : at + 8
                        ]
        done = pl.ds(part * TG * PAIRS * 8, TG * PAIRS * 8)
        out[done, :] = merged[done, :].astype(BF16)

    for part in range(PARTS):
        others(lambda g: deliver(g, part).wait_send())

    lax.fori_loop(5, Z - 1, drain_hops, 0)

    @pl.when(jnp.logical_or(to_low, to_high))
    def _():
        def each(g, _):
            for part in range(PARTS):
                edge(g, part, hour, 0).wait_send()
            return 0

        lax.fori_loop(0, GROUPS, each, 0)


def local(spectra, smooth_kernel, owner_ids, turn_order, source_pick, receiver_pick):
    tiles = spectra.reshape(HOURS_DEV, C_DEV, 2, NB, BAND)
    tiles = tiles.transpose(0, 1, 3, 2, 4).reshape(TILE_ROWS, BAND)
    vmem = pl.BlockSpec(memory_space=pltpu.VMEM)
    hbm = pl.BlockSpec(memory_space=pltpu.HBM)
    rows = TURNS * 2 * PAIRS
    dma = pltpu.SemaphoreType.DMA
    result = pl.pallas_call(
        body,
        out_shape=pltpu.VMEM((rows * 4, BAND), BF16),
        in_specs=[hbm] * 6,
        out_specs=vmem,
        scratch_shapes=[
            pltpu.VMEM((TILE_ROWS + 64, BAND), F32),
            pltpu.VMEM((NB, ROWS, BAND), BF16),
            pltpu.VMEM((GROUPS, HOUR_DEVS, ROWS, BAND), BF16),
            pltpu.VMEM((Z, TURNS, ROWS, BAND), BF16),
            pltpu.VMEM((Z, TURNS, ROWS, BAND), BF16),
            pltpu.VMEM((TURNS, 2, ROWS, BAND), F32),
            pltpu.VMEM((GROUPS, TURNS, 8, 3, 8, BAND), F32),
            pltpu.VMEM((GROUPS, 2 * PAIRS, BAND), BF16),
            pltpu.VMEM((GROUPS, rows, BAND), BF16),
            pltpu.VMEM((6, rows, BAND), BF16),
            pltpu.VMEM((rows * 4 + 64, BAND), F32),
            pltpu.VMEM((3, 4, BAND, BAND), BF16),
            pltpu.SMEM((TURNS,), jnp.int32),
            pltpu.SMEM((TURNS,), jnp.int32),
            pltpu.VMEM((1, PAIRS), jnp.int32),
            pltpu.VMEM((1, PAIRS), jnp.int32),
            dma((6,)),
            dma((NB,)),
            dma((GROUPS, HOUR_DEVS)),
            dma((Z, PARTS)),
            dma((Z, PARTS)),
            dma((Z, PARTS)),
            dma((Z, PARTS)),
            dma((GROUPS,)),
            dma((GROUPS,)),
            dma((GROUPS, PARTS)),
            dma((6, PARTS)),
            dma((GROUPS, PARTS)),
        ],
        compiler_params=pltpu.CompilerParams(
            collective_id=0, has_side_effects=True, vmem_limit_bytes=63 * 1024 * 1024
        ),
    )(
        tiles,
        smooth_kernel,
        owner_ids,
        turn_order,
        source_pick.reshape(1, PAIRS),
        receiver_pick.reshape(1, PAIRS),
    )
    result = result.reshape(TURNS, PAIRS, 4, 2, BAND).transpose(0, 1, 3, 2, 4)
    return result.reshape(TURNS, PAIRS, 2, 4 * BAND)


def solution(mesh):
    return jax.shard_map(
        local,
        mesh=mesh,
        in_specs=(
            P("hour", "chan", None, None),
            P(None, "hour", None, None),
            P(),
            P(),
            P("chan"),
            P("chan"),
        ),
        out_specs=P(None, "chan", None, "hour"),
        check_vma=False,
    )
```

```python
import jax
import jax.numpy as jnp
from jax import lax
from jax.experimental import pallas as pl
from jax.experimental.pallas import tpu as pltpu
from jax.sharding import PartitionSpec as P

MESH = pl.DeviceIdType.MESH

BAND = 128
TURNS = 4
C_DEV = 8
PAIRS = 32
HOUR_DEVS = 8
HOURS_DEV = 6
Z = 8
GROUPS = 4
ROWS = HOURS_DEV * 16
TG = 2
PARTS = TURNS // TG
FIRST = 24
NB = 32
TILE_ROWS = HOURS_DEV * C_DEV * NB * 2
BF16 = jnp.bfloat16
F32 = jnp.float32


def body(
    spectra, kernel_hbm, owners_hbm, order_hbm, source_hbm, receiver_hbm, out,
    raw, staged, recv, up, down, chosen, acc, onehot, picked, halo, merged,
    kernel, owner_ids, turn_order, source_pick, receiver_pick, load_sem,
    a2a_send, a2a_recv, up_send, up_recv, down_send, down_recv,
    hot_send, hot_recv, out_send, out_recv, edge_send,
):
    chan = lax.axis_index("chan")
    hour = lax.axis_index("hour")
    core = chan % 2
    z = (chan // 2) % Z
    y_hi = chan // (2 * Z)
    group = y_hi * 2 + core

    def chan_of(g, level):
        return ((g // 2) * Z + level) * 2 + g % 2

    loads = [
        pltpu.make_async_copy(a, b, load_sem.at[n])
        for n, (a, b) in enumerate(
            [
                (spectra, raw.at[pl.ds(0, TILE_ROWS)]),
                (owners_hbm, owner_ids),
                (order_hbm, turn_order),
                (source_hbm, source_pick),
                (receiver_hbm, receiver_pick),
                (kernel_hbm, kernel),
            ]
        )
    ]
    for load in loads:
        load.start()

    barrier = pltpu.get_barrier_semaphore()

    def greet(n, _):
        g, h = n // HOUR_DEVS, n % HOUR_DEVS

        @pl.when(jnp.logical_or(g != group, h != hour))
        def _():
            pl.semaphore_signal(
                barrier, inc=1, device_id=(chan_of(g, z), h), device_id_type=MESH
            )

        return 0

    above = chan_of(group, (z + 1) % Z)
    below = chan_of(group, (z + Z - 1) % Z)
    lax.fori_loop(0, NB, greet, 0)
    pl.semaphore_signal(barrier, inc=1, device_id=(above, hour), device_id_type=MESH)
    pl.semaphore_signal(barrier, inc=1, device_id=(below, hour), device_id_type=MESH)

    for load in loads[3:5]:
        load.wait()

    src = source_pick[...]
    rec = receiver_pick[...]
    code = (((rec - src) & 7) * 16 + src).astype(F32)
    row = lax.broadcasted_iota(jnp.int32, (PAIRS, PAIRS), 0)
    col = lax.broadcasted_iota(jnp.int32, (PAIRS, PAIRS), 1)
    spread = jnp.where(row == col, jnp.broadcast_to(code, (PAIRS, PAIRS)), 0.0)
    code_col = jnp.sum(spread, axis=1, keepdims=True)
    lane = lax.broadcasted_iota(jnp.int32, (PAIRS, BAND), 1).astype(F32)
    for c in range(2):
        hot = jnp.where(lane == code_col + 8.0 * c, 1.0, 0.0)
        onehot[group, pl.ds(c * PAIRS, PAIRS), :] = hot.astype(BF16)

    acc[...] = jnp.zeros_like(acc)

    @pl.when(hour == 0)
    def _():
        halo[0] = jnp.zeros((2 * TURNS * PAIRS, BAND), BF16)

    @pl.when(hour == HOUR_DEVS - 1)
    def _():
        halo[5] = jnp.zeros((2 * TURNS * PAIRS, BAND), BF16)

    for load in loads[:3]:
        load.wait()
    pl.semaphore_wait(barrier, NB + 1)

    def a2a(g, h):
        band = h * GROUPS + g
        return pltpu.make_async_remote_copy(
            src_ref=staged.at[band],
            dst_ref=recv.at[group, hour],
            send_sem=a2a_send.at[band],
            recv_sem=a2a_recv.at[group, hour],
            device_id=(chan_of(g, z), h),
            device_id_type=MESH,
        )

    def shift_of(q):
        q = (q + 2 * Z) % Z
        return q // 4, q % 4

    def hour_of(q):
        far, along = shift_of(q)
        return (hour // 4 + far) % 2 * 4 + (hour + along) % 4

    def hour_for(q):
        far, along = shift_of(q)
        return (hour // 4 + far) % 2 * 4 + (hour + 4 - along) % 4

    def target(n):
        k = n // GROUPS
        g = (group + n) % GROUPS
        step = (k + 1) // 2
        shift = jnp.where(k % 2 == 1, step, 2 * Z - step)
        return g, hour_for(z + shift)

    def scatter(n, _):
        g, h = target(n)
        band = h * GROUPS + g
        mine = jnp.logical_and(g == group, h == hour)
        for i in range(HOURS_DEV):
            parts = [
                raw[pl.ds(i * 512 + band * 2 + p, 8, stride=64), :] for p in range(2)
            ]
            staged[band, pl.ds(i * 16, 16), :] = jnp.concatenate(parts, 0).astype(BF16)

        @pl.when(jnp.logical_not(mine))
        def _():
            a2a(g, h).start()

        @pl.when(mine)
        def _():
            recv[group, hour] = staged[band]

        return 0

    def drain(n, _):
        g, h = target(n)

        @pl.when(jnp.logical_or(g != group, h != hour))
        def _():
            a2a(g, h).wait_send()

        return 0

    lax.fori_loop(0, FIRST, scatter, 0)

    def hot_copy(g):
        return pltpu.make_async_remote_copy(
            src_ref=onehot.at[group],
            dst_ref=onehot.at[group],
            send_sem=hot_send.at[g],
            recv_sem=hot_recv.at[group],
            device_id=(chan_of(g, z), hour),
            device_id_type=MESH,
        )

    def hot_wait(g):
        return pltpu.make_async_remote_copy(
            src_ref=onehot.at[group],
            dst_ref=onehot.at[g],
            send_sem=hot_send.at[g],
            recv_sem=hot_recv.at[g],
            device_id=(chan_of(g, z), hour),
            device_id_type=MESH,
        )

    def others(fn):
        def each(n, _):
            fn((group + n) % GROUPS)
            return 0

        lax.fori_loop(1, GROUPS, each, 0)


    owners = [owner_ids[turn_order[t]] for t in range(TURNS)]
    owner_z = [(o // 2) % Z for o in owners]
    owner_g = [(o // (2 * Z)) * 2 + o % 2 for o in owners]

    def wait_pieces(h):
        def each(g, _):
            @pl.when(jnp.logical_or(g != group, h != hour))
            def _():
                pltpu.make_async_remote_copy(
                    src_ref=staged.at[0],
                    dst_ref=recv.at[g, h],
                    send_sem=a2a_send.at[0],
                    recv_sem=a2a_recv.at[g, h],
                    device_id=(chan_of(g, z), h),
                    device_id_type=MESH,
                ).wait_recv()

            return 0

        lax.fori_loop(0, GROUPS, each, 0)

    def merge(buf, s, h, t0, first):
        for i in range(HOURS_DEV):
            rows = pl.ds(i * 16, 16)
            held = [recv[g, h, rows, :] for g in range(GROUPS)]
            for t in range(t0, t0 + TG):
                mine = held[0]
                for g in range(1, GROUPS):
                    mine = lax.select_n(owner_g[t] == g, mine, held[g])
                if not first:
                    mine = lax.select_n(owner_z[t] == z, buf[s, t, rows, :], mine)
                buf[s, t, rows, :] = mine

    def hop(buf, s, part, send, arrive, target):
        turns = pl.ds(part * TG, TG)
        return pltpu.make_async_remote_copy(
            src_ref=buf.at[s, turns],
            dst_ref=buf.at[s + 1, turns],
            send_sem=send.at[s, part],
            recv_sem=arrive.at[s + 1, part],
            device_id=(target, hour),
            device_id_type=MESH,
        )

    def arrived(buf, s, part, send, arrive, source):
        turns = pl.ds(part * TG, TG)
        pltpu.make_async_remote_copy(
            src_ref=buf.at[0, turns],
            dst_ref=buf.at[s, turns],
            send_sem=send.at[0, part],
            recv_sem=arrive.at[s, part],
            device_id=(source, hour),
            device_id_type=MESH,
        ).wait_recv()

    def choose(r, slot, turns):
        q = z - r + 2 * Z
        for t in turns:
            position = (owner_z[t] + 4 * Z - q) % Z
            lower = position < jnp.maximum(r, 1)
            for i in range(HOURS_DEV):
                rows = pl.ds(i * 16, 16)
                value = lax.select_n(
                    lower, down[Z - 1 - r, t, rows, :], up[r, t, rows, :]
                )
                chosen[t, slot, rows, :] = value.astype(F32)

    def multiply(g, t0, hours):
        for k0 in range(0, 8, 4):
            span = range(k0, k0 + 4)
            sums = [acc[g, t0 + t, k, c] for t in range(2) for k in span for c in range(3)]
            for slot in range(2):
                for i in range(HOURS_DEV):
                    rows = pl.ds(i * 16, 16)
                    b = recv[g, hours[slot], rows, :].astype(F32)
                    b0, b1 = b[:8], b[8:]
                    a = [chosen[t0 + t, slot, rows, :] for t in range(2)]
                    a = [(x[:8], x[8:], x[:8] + x[8:]) for x in a]
                    for k in span:
                        r0 = pltpu.roll(b0, 8 - k, 0) if k else b0
                        r1 = pltpu.roll(b1, 8 - k, 0) if k else b1
                        rd = r0 - r1
                        for t in range(2):
                            at = (t * 4 + k - k0) * 3
                            sums[at] = sums[at] + a[t][0] * r0
                            sums[at + 1] = sums[at + 1] + a[t][1] * r1
                            sums[at + 2] = sums[at + 2] + a[t][2] * rd
            n = 0
            for t in range(2):
                for k in span:
                    for c in range(3):
                        acc[g, t0 + t, k, c] = sums[n]
                        n += 1

    def table_of(g, t):
        parts = []
        for k in range(8):
            real, imag, cross = (acc[g, t, k, c] for c in range(3))
            parts += [real + imag, cross - real + imag]
        return jnp.concatenate(parts, axis=0).astype(BF16)

    def climb(s, part, first=False):
        if not first:
            arrived(up, s, part, up_send, up_recv, below)
        merge(up, s, hour_of(z - s), part * TG, first)
        hop(up, s, part, up_send, up_recv, above).start()

    def descend(s, part, first=False):
        if not first:
            arrived(down, s, part, down_send, down_recv, above)
        merge(down, s, hour_of(z + 1 + s), part * TG, first)
        hop(down, s, part, down_send, down_recv, below).start()

    def step(s):
        for part in range(PARTS):
            climb(s, part)
        for part in range(PARTS):
            descend(s, part)

    def early(s, _):
        wait_pieces(hour_of(z - s))
        for part in range(PARTS):
            climb(s, part)
        wait_pieces(hour_of(z + 1 + s))
        for part in range(PARTS):
            descend(s, part)
        lax.fori_loop(s * 8 - 8, s * 8, drain, 0)
        return 0

    def drain_hops(s, _):
        for part in range(PARTS):
            hop(up, s, part, up_send, up_recv, above).wait_send()
            hop(down, s, part, down_send, down_recv, below).wait_send()
        return 0

    def late(s, _):
        step(s)
        low, high = hour_of(z - s), hour_of(z + 1 + s)
        choose(s, 0, range(TURNS))
        choose(Z - 1 - s, 1, range(TURNS))

        def each(n, _):
            multiply(n // 2, (n % 2) * 2, (low, high))
            return 0

        lax.fori_loop(0, GROUPS * 2, each, 0)
        drain_hops(s - 2, 0)
        return 0

    wait_pieces(hour_of(z))
    for part in range(PARTS):
        climb(0, part, True)
    wait_pieces(hour_of(z + 1))
    for part in range(PARTS):
        descend(0, part, True)
    lax.fori_loop(FIRST, NB, scatter, 0)
    others(lambda g: hot_copy(g).start())
    lax.fori_loop(1, 4, early, 0)
    lax.fori_loop(NB * 3 // 4, NB, drain, 0)
    others(lambda g: hot_copy(g).wait_send())
    lax.fori_loop(0, 2, drain_hops, 0)
    lax.fori_loop(4, Z - 1, late, 0)
    low, high = hour_of(z + 1), hour_of(z)
    others(lambda g: hot_wait(g).wait_recv())

    def deliver(g, part):
        rows = pl.ds(part * TG * 2 * PAIRS, TG * 2 * PAIRS)
        return pltpu.make_async_remote_copy(
            src_ref=picked.at[g, rows],
            dst_ref=halo.at[1 + group, rows],
            send_sem=out_send.at[g, part],
            recv_sem=out_recv.at[1 + group, part],
            device_id=(chan_of(g, z), hour),
            device_id_type=MESH,
        )

    def edge(g, part, to, slot):
        rows = pl.ds(part * TG * 2 * PAIRS, TG * 2 * PAIRS)
        return pltpu.make_async_remote_copy(
            src_ref=picked.at[g, rows],
            dst_ref=halo.at[slot, rows],
            send_sem=edge_send.at[g, part],
            recv_sem=out_recv.at[slot, part],
            device_id=(chan_of(g, z), to),
            device_id_type=MESH,
        )

    to_low = jnp.logical_and(group == 0, hour > 0)
    to_high = jnp.logical_and(group == GROUPS - 1, hour < HOUR_DEVS - 1)

    for part in range(PARTS):
        turns = range(part * TG, part * TG + TG)
        arrived(up, Z - 1, part, up_send, up_recv, below)
        arrived(down, Z - 1, part, down_send, down_recv, above)
        choose(Z - 1, 0, turns)
        choose(0, 1, turns)

        def finish(n, _, part=part, turns=turns):
            g = (group + 1 + n) % GROUPS
            for t in turns[::2]:
                multiply(g, t, (low, high))
            table = jnp.concatenate(
                [
                    table_of(g, t)
                    for t in turns
                ],
                axis=1,
            )
            rows = jnp.dot(onehot[g], table, preferred_element_type=F32).astype(BF16)
            for n2, t in enumerate(turns):
                picked[g, pl.ds(t * 2 * PAIRS, 2 * PAIRS), :] = rows[
                    :, n2 * BAND : (n2 + 1) * BAND
                ]

            @pl.when(g != group)
            def _():
                deliver(g, part).start()

            @pl.when(g == group)
            def _():
                rows = pl.ds(part * TG * 2 * PAIRS, TG * 2 * PAIRS)
                halo[1 + group, rows, :] = picked[g, rows, :]

            @pl.when(to_low)
            def _():
                edge(g, part, hour - 1, 5).start()

            @pl.when(to_high)
            def _():
                edge(g, part, hour + 1, 0).start()

            return 0

        lax.fori_loop(0, GROUPS, finish, 0)

    def out_wait(slot, part):
        rows = pl.ds(part * TG * 2 * PAIRS, TG * 2 * PAIRS)
        pltpu.make_async_remote_copy(
            src_ref=picked.at[0, rows],
            dst_ref=halo.at[slot, rows],
            send_sem=out_send.at[0, part],
            recv_sem=out_recv.at[slot, part],
            device_id=(chan, hour),
            device_id_type=MESH,
        ).wait_recv()

    lax.fori_loop(5, Z - 1, drain_hops, 0)

    loads[5].wait()
    for part in range(PARTS):
        others(lambda g: out_wait(1 + g, part))

        @pl.when(hour > 0)
        def _():
            out_wait(0, part)

        @pl.when(hour < HOUR_DEVS - 1)
        def _():
            out_wait(5, part)

        rows = pl.ds(part * TG * 2 * PAIRS, TG * 2 * PAIRS)
        for b in range(4):
            total = jnp.dot(halo[b, rows, :], kernel[0, b], preferred_element_type=F32)
            for d in range(1, 3):
                total += jnp.dot(
                    halo[b + d, rows, :], kernel[d, b], preferred_element_type=F32
                )
            for t in range(TG):
                for c in range(2):
                    for p in range(0, PAIRS, 8):
                        at = t * 2 * PAIRS + c * PAIRS + p
                        pair = (part * TG + t) * PAIRS + p
                        merged[pl.ds(pair * 8 + b * 2 + c, 8, stride=8), :] = total[
                            at : at + 8
                        ]
        done = pl.ds(part * TG * PAIRS * 8, TG * PAIRS * 8)
        out[done, :] = merged[done, :].astype(BF16)

    for part in range(PARTS):
        others(lambda g: deliver(g, part).wait_send())


    @pl.when(jnp.logical_or(to_low, to_high))
    def _():
        def each(g, _):
            for part in range(PARTS):
                edge(g, part, hour, 0).wait_send()
            return 0

        lax.fori_loop(0, GROUPS, each, 0)


def local(spectra, smooth_kernel, owner_ids, turn_order, source_pick, receiver_pick):
    tiles = spectra.reshape(HOURS_DEV, C_DEV, 2, NB, BAND)
    tiles = tiles.transpose(0, 1, 3, 2, 4).reshape(TILE_ROWS, BAND)
    vmem = pl.BlockSpec(memory_space=pltpu.VMEM)
    hbm = pl.BlockSpec(memory_space=pltpu.HBM)
    rows = TURNS * 2 * PAIRS
    dma = pltpu.SemaphoreType.DMA
    result = pl.pallas_call(
        body,
        out_shape=pltpu.VMEM((rows * 4, BAND), BF16),
        in_specs=[hbm] * 6,
        out_specs=vmem,
        scratch_shapes=[
            pltpu.VMEM((TILE_ROWS + 64, BAND), F32),
            pltpu.VMEM((NB, ROWS, BAND), BF16),
            pltpu.VMEM((GROUPS, HOUR_DEVS, ROWS, BAND), BF16),
            pltpu.VMEM((Z, TURNS, ROWS, BAND), BF16),
            pltpu.VMEM((Z, TURNS, ROWS, BAND), BF16),
            pltpu.VMEM((TURNS, 2, ROWS, BAND), F32),
            pltpu.VMEM((GROUPS, TURNS, 8, 3, 8, BAND), F32),
            pltpu.VMEM((GROUPS, 2 * PAIRS, BAND), BF16),
            pltpu.VMEM((GROUPS, rows, BAND), BF16),
            pltpu.VMEM((6, rows, BAND), BF16),
            pltpu.VMEM((rows * 4 + 64, BAND), F32),
            pltpu.VMEM((3, 4, BAND, BAND), BF16),
            pltpu.SMEM((TURNS,), jnp.int32),
            pltpu.SMEM((TURNS,), jnp.int32),
            pltpu.VMEM((1, PAIRS), jnp.int32),
            pltpu.VMEM((1, PAIRS), jnp.int32),
            dma((6,)),
            dma((NB,)),
            dma((GROUPS, HOUR_DEVS)),
            dma((Z, PARTS)),
            dma((Z, PARTS)),
            dma((Z, PARTS)),
            dma((Z, PARTS)),
            dma((GROUPS,)),
            dma((GROUPS,)),
            dma((GROUPS, PARTS)),
            dma((6, PARTS)),
            dma((GROUPS, PARTS)),
        ],
        compiler_params=pltpu.CompilerParams(
            collective_id=0, has_side_effects=True, vmem_limit_bytes=63 * 1024 * 1024
        ),
    )(
        tiles,
        smooth_kernel,
        owner_ids,
        turn_order,
        source_pick.reshape(1, PAIRS),
        receiver_pick.reshape(1, PAIRS),
    )
    result = result.reshape(TURNS, PAIRS, 4, 2, BAND).transpose(0, 1, 3, 2, 4)
    return result.reshape(TURNS, PAIRS, 2, 4 * BAND)


def solution(mesh):
    return jax.shard_map(
        local,
        mesh=mesh,
        in_specs=(
            P("hour", "chan", None, None),
            P(None, "hour", None, None),
            P(),
            P(),
            P("chan"),
            P("chan"),
        ),
        out_specs=P(None, "chan", None, "hour"),
        check_vma=False,
    )
```
